32 devices in a mesh: groups: 2 (over x), shard: 8 (over z, y), sub: 2 (over core).
Axes of the slice: x: 2, y: 2, z: 4, core: 2. Of those that a mesh axis runs over, the one named last changes fastest.
Arguments:
- queries: bfloat16 [256, 32, 128], P(('groups', 'shard'), 'sub'), parts along dimension 0, may hold values from -6 to 6
- candidates: int32 [256, 16], P(('groups', 'shard')), parts along dimension 0, may hold values from 0 to 1023, as said below
- residuals: int32 [1024, 128, 16], P(('shard', 'sub')), may hold values from 0 to 65535, as said below
- centroid_ids: int32 [1024, 128], P(('shard', 'sub')), may hold values from 0 to 4095
- block_scales: bfloat16 [1024, 128], P(('shard', 'sub')), may hold values from 0.25 to 1
- lengths: int32 [1024], P(('shard', 'sub')), may hold values from 17 to 128
- centroids: bfloat16 [4096, 128], replicated, may hold values from -0.5 to 0.5
- bucket_weights: bfloat16 [4], replicated, may hold values from -0.25 to 0.25
Outputs:
- scores: float32 [256, 16], P(('groups', 'shard')), parts along dimension 0
The draws below stay inside these ranges and needn't reach their ends.
There are 2 independent parts, one for each index of `groups`. The reference program is written for one: setup_inputs(seed, part) draws one part's arguments, and reference() takes and returns one part's arrays. A program takes and returns all parts, laid end to end along the dimension named above; an argument that names none is the same for every part. Nothing has to cross between parts.
Inputs may be any that keep to these rules, and one draw needn't show every extreme that they name: `candidates`: each id names a passage; passage p lies on device p // 64 of shard+sub. Among the 256 pairs of one block of 16 queries (one index of shard), at most 32 name passages of any one device; in every draw one device receives exactly 32 pairs from every block. `residuals`: each word packs 8 independent 2-bit codes, code e % 8 in bits 2 * (e % 8) and 2 * (e % 8) + 1; higher bits are zero.
All inputs are finite; a program needn't handle non-finite values.
Results may differ from the reference program's by a relative error of at most 0.0003.
Values may be sent and summed in bfloat16 or wider, within the bound.
No kernel may reach another device: no remote copies, remote signals or barrier semaphores. Data moves between devices by JAX's collectives and lax.ppermute only.
A program may use at most 64 MiB of HBM per device.

```python
import math
import jax
import jax.numpy as jnp
from jax import lax

D = 128
QT = 32
PLEN = 128
CENT = 4096
K = 16
QDEV = 16
PDEV = 64
NQ = 128
NPASS = 1024
CAP = 32


def draw_candidates(key, part):
    key = jax.random.fold_in(key, 11)
    device_count = NPASS // PDEV
    pair_count = QDEV * K
    block_count = NQ // QDEV
    hottest = jax.random.randint(jax.random.fold_in(key, 1), (), 0, device_count)

    def one_block(block_key):
        cell_key, order_key, local_key = jax.random.split(block_key, 3)
        cells = jax.random.permutation(cell_key, (device_count - 1) * CAP)[:pair_count - CAP]
        others = (cells // CAP).astype(jnp.int32)
        others = others + (others >= hottest).astype(jnp.int32)
        targets = jnp.concatenate([jnp.full((CAP,), hottest, jnp.int32), others])
        targets = jax.random.permutation(order_key, targets)
        local_ids = jax.random.randint(local_key, (pair_count,), 0, PDEV)
        return (targets * PDEV + local_ids).reshape(QDEV, K)
    blocks = jax.vmap(one_block)(jax.random.split(jax.random.fold_in(key, 2), block_count))
    return blocks.reshape(NQ, K).astype(jnp.int32)


def draw_residuals(key, part):
    key = jax.random.fold_in(key, 5)
    codes = jax.random.randint(key, (NPASS, PLEN, D // 8, 8), 0, 4).astype(jnp.int32)
    shifts = 2 * jnp.arange(8, dtype=jnp.int32)
    return jnp.sum(jnp.left_shift(codes, shifts), axis=-1, dtype=jnp.int32).astype(jnp.int32)


def with_ends(array, stream_key, low, high):
    spot = [jax.random.randint(jax.random.fold_in(stream_key, axis), (), 0, length) for axis, length in enumerate(array.shape)]
    longest = array.shape.index(max(array.shape))
    neighbour = spot[:longest] + [(spot[longest] + 1) % array.shape[longest]] + spot[longest + 1:]
    return array.at[tuple(spot)].set(low).at[tuple(neighbour)].set(high)


def block_scale(rng, shape, cuts, smallest, largest):
    gain = 1.0
    for dim, parts in cuts:
        heights = jax.random.uniform(jax.random.fold_in(jax.random.fold_in(rng, 6), dim), (parts,), jnp.float32, smallest / len(cuts), largest / len(cuts))
        gain = gain * jnp.repeat(jnp.exp(heights), shape[dim] // parts).reshape((-1,) + (1,) * (len(shape) - 1 - dim))
    return gain


def bell_draw(stream_key, shape, deviation, most, cuts=(), kind=jnp.bfloat16):
    values = jax.random.normal(stream_key, shape, jnp.float32) * deviation
    if len(cuts) > 0:
        values = block_scale(stream_key, shape, cuts, -0.22, 0.18) * values
    return jnp.clip(values, min=-most, max=most).astype(kind)


def setup_inputs(seed: int = 0, part: int = 0) -> dict:
    arg_keys = jax.random.split(jax.random.key(seed), 9)
    part_splits = jax.random.split(jax.random.fold_in(arg_keys[8], part), 9)
    queries = bell_draw(part_splits[0], (NQ, QT, D), 1.0, 6.0, ((0, 8), (1, 2)))
    candidates = draw_candidates(jax.random.fold_in(jax.random.fold_in(arg_keys[8], part), 71), part)
    residuals = draw_residuals(jax.random.fold_in(arg_keys[8], 71), part)
    centroid_ids = with_ends(jax.random.randint(arg_keys[3], (NPASS, PLEN), 0, CENT), jax.random.fold_in(arg_keys[3], 1), 0, CENT - 1).astype(jnp.int32)
    block_scales = jnp.clip(jnp.exp(math.log(1.0) - 1.3862944 * jax.random.uniform(arg_keys[4], (NPASS, PLEN), jnp.float32) ** block_scale(arg_keys[4], (NPASS, PLEN), ((0, 16),), -0.2, 0.2)), 0.25, 1.0).astype(jnp.bfloat16)
    lengths = with_ends(jax.random.randint(arg_keys[5], (NPASS,), PLEN // 8 + 1, PLEN + 1), jax.random.fold_in(arg_keys[5], 1), PLEN // 8 + 1, PLEN).astype(jnp.int32)
    centroids = bell_draw(arg_keys[6], (CENT, D), D ** -0.5, 0.5)
    bucket_weights = jnp.clip(jax.random.uniform(arg_keys[7], (4,), jnp.float32, -0.25, 0.25), -0.25, 0.25).astype(jnp.bfloat16)
    return dict(queries=queries, candidates=candidates, residuals=residuals, centroid_ids=centroid_ids, block_scales=block_scales, lengths=lengths, centroids=centroids, bucket_weights=bucket_weights)


masked_floor = -1000000000.0

def decode_tokens(packed, ids_here, scales_here, centroids, buckets):
    shifts = 2 * jnp.arange(8, dtype=jnp.int32)
    codes = jnp.bitwise_and(jnp.right_shift(packed[..., None], shifts), 3)
    codes = codes.reshape(packed.shape[:-1] + (packed.shape[-1] * 8,))
    levels = jnp.arange(4, dtype=jnp.int32)
    values = lax.optimization_barrier(jnp.sum(jnp.where(codes[..., None] == levels, buckets.astype(jnp.float32), jnp.float32(0.0)), axis=-1))
    centre = jnp.take(centroids, ids_here, axis=0).astype(jnp.float32)
    summed = centre + scales_here.astype(jnp.float32)[..., None] * values
    inverse = lax.rsqrt(lax.optimization_barrier(jnp.sum(summed * summed, axis=-1, keepdims=True)) + 1e-06)
    return (summed * inverse).astype(jnp.bfloat16)

def reference(queries, candidates, residuals, centroid_ids, block_scales, lengths, centroids, bucket_weights):

    def one_query(operands):
        query_rows, picked = operands
        embedded = decode_tokens(residuals[picked], centroid_ids[picked], block_scales[picked], centroids, bucket_weights)
        similar = jnp.einsum('kpd,td->ktp', embedded.astype(jnp.float32), query_rows.astype(jnp.float32))
        positions = lax.broadcasted_iota(jnp.int32, similar.shape, 2)
        living = positions < lengths[picked][:, None, None]
        best_match = lax.optimization_barrier(jnp.max(jnp.where(living, similar, masked_floor), axis=2))
        return lax.optimization_barrier(jnp.sum(best_match, axis=1)) / QT
    return lax.map(one_query, (queries, candidates))
```

```python
import functools

import jax
import jax.numpy as jnp
from jax import lax
from jax.experimental import pallas as pl
from jax.experimental.pallas import tpu as pltpu
from jax.sharding import PartitionSpec as P

masked_floor = -1000000000.0
VMEM = pltpu.VMEM
SMEM = pltpu.SMEM
LIMIT = pltpu.CompilerParams(vmem_limit_bytes=40 * 2**20)


def iota(shape, dim):
    return lax.broadcasted_iota(jnp.int32, shape, dim)


def ones_where(mask):
    return jnp.where(mask, 1.0, 0.0).astype(jnp.bfloat16)


def dot(a, b, contract=((1,), (0,))):
    return lax.dot_general(a, b, (contract, ((), ())), preferred_element_type=jnp.float32)


def spread(feature, words, per):
    return per * (feature % words) + feature // words


def pack_kernel(words, passages, query_ref, cand_ref, out_ref):
    count, tokens, width = query_ref.shape
    per = width // words
    order = ones_where(iota((width, width), 0) == spread(iota((width, width), 1), words, per))
    flat = query_ref[...].reshape(count * tokens, width)
    rows = count * tokens
    out_ref[0:rows, :] = dot(flat, order).astype(jnp.bfloat16)
    picks = cand_ref.shape[1]
    repeat = ones_where(iota((picks, width), 0) == iota((picks, width), 1) % picks)
    ids = cand_ref[...]
    owner = ids // passages
    local = ids - owner * passages
    for i, part in enumerate((owner, local)):
        part = part.astype(jnp.float32).astype(jnp.bfloat16)
        out_ref[rows + i * count : rows + (i + 1) * count, :] = dot(part, repeat).astype(jnp.bfloat16)


def decode_kernel(ids_ref, len_ref, words_ref, scale_ref, table_ref, bucket_ref, out_ref, wide, rows):
    count, slots = ids_ref.shape
    entries, width = table_ref.shape
    words = words_ref.shape[1]
    per = width // words
    chunk = 512

    def widen(i, _):
        r = pl.ds(pl.multiple_of(i * chunk, chunk), chunk)
        wide[r, :] = table_ref[r, :].astype(jnp.float32)
        return 0

    lax.fori_loop(0, entries // chunk, widen, 0)
    order = ones_where(iota((width, width), 1) == spread(iota((width, width), 0), words, per))
    eye = iota((slots, slots), 0) == iota((slots, slots), 1)
    levels = [
        jnp.broadcast_to(bucket_ref[0:1, i : i + 1].astype(jnp.float32), (words, slots))
        for i in range(4)
    ]

    def fetch(p, buf):
        for g in range(slots // 16):
            got = jnp.concatenate(
                [wide[pl.ds(ids_ref[p, g * 16 + i], 1), :] for i in range(16)], axis=0
            )
            rows[buf, g * 16 : (g + 1) * 16, :] = got.astype(jnp.bfloat16)

    def build(p, buf):
        packed = words_ref[p]
        parts = []
        for k in range(per):
            low = (packed & (1 << (2 * k))) != 0
            high = (packed & (2 << (2 * k))) != 0
            parts.append(
                jnp.where(
                    high,
                    jnp.where(low, levels[3], levels[2]),
                    jnp.where(low, levels[1], levels[0]),
                )
            )
        value = jnp.concatenate(parts, axis=0)
        scale = scale_ref[pl.ds(p, 1), :]
        raw = dot(order, rows[buf], ((1,), (1,))) + scale * value
        inverse = lax.rsqrt(jnp.sum(raw * raw, axis=0, keepdims=True) + 1e-06)
        out_ref[p] = (raw * inverse).astype(jnp.bfloat16)

    fetch(0, 0)

    def step(i, _):
        fetch(2 * i + 1, 1)
        build(2 * i, 0)
        fetch(jnp.minimum(2 * i + 2, count - 1), 0)
        build(2 * i + 1, 1)
        return 0

    lax.fori_loop(0, count // 2, step, 0)


def pair_kernel(
    queries, picks, capacity, me_ref, len_ref, mine_ref, other_ref, emb_ref, out_ref, slot_v, slot_s, score, sem
):
    blocks = mine_ref.shape[0]
    width = mine_ref.shape[2]
    tokens = (mine_ref.shape[1] - 2 * queries) // queries
    body_rows = queries * tokens
    groups = width // picks
    rows = blocks * queries
    owner = mine_ref[:, body_rows : body_rows + queries, :].reshape(rows, width).astype(jnp.float32)
    local = (
        mine_ref[:, body_rows + queries : body_rows + 2 * queries, :]
        .reshape(rows, width)
        .astype(jnp.float32)
    )
    here = owner == me_ref[0].astype(jnp.float32)
    here_bf = ones_where(here)
    li = iota((width, width), 0)
    lj = iota((width, width), 1)
    before_lane = ones_where((li < picks) & (li < lj % picks))
    whole_row = ones_where(li < picks)
    ri = iota((rows, rows), 0)
    rj = iota((rows, rows), 1)
    before_row = ones_where((ri // queries == rj // queries) & (rj < ri))
    totals = dot(here_bf, whole_row).astype(jnp.bfloat16)
    rank = dot(here_bf, before_lane) + dot(before_row, totals)
    rank = rank.astype(jnp.int32)
    lane_group = iota((rows, width), 1) // picks
    which = (iota((rows, width), 0) % queries).astype(jnp.float32)
    padded = slot_v.shape[0] // 2
    collect = ones_where(iota((padded, rows), 0) == iota((padded, rows), 1) // queries)
    slot_q = jnp.zeros((padded, width), jnp.float32)
    slot_p = jnp.zeros((padded, width), jnp.float32)
    for i in range(-(-capacity // groups)):
        chosen = here & (rank == i * groups + lane_group)
        to_slot = ones_where(lj == i * groups + li // picks)
        got_q = dot(collect, jnp.where(chosen, which, 0.0).astype(jnp.bfloat16))
        got_p = dot(collect, jnp.where(chosen, local, 0.0).astype(jnp.bfloat16))
        slot_q += dot(got_q.astype(jnp.bfloat16), to_slot)
        slot_p += dot(got_p.astype(jnp.bfloat16), to_slot)
    slot_v[0:padded, :] = slot_q.astype(jnp.int32)
    slot_v[padded : 2 * padded, :] = slot_p.astype(jnp.int32)
    copy = pltpu.make_async_copy(slot_v, slot_s, sem)
    copy.start()
    copy.wait()

    lane = iota((2 * tokens, width), 1)
    full_tokens = 2 * tokens

    def block(b, _):
        best_all = jnp.zeros((full_tokens, width), jnp.float32)
        for s in range(capacity):
            p = slot_s[padded + b, s]
            r = pl.ds(pl.multiple_of(slot_s[b, s] * tokens, tokens), tokens)
            rows_q = jnp.concatenate([mine_ref[b, r, :], other_ref[b, r, :]], axis=0)
            similar = dot(rows_q, emb_ref[p])
            similar = jnp.where(lane < len_ref[p], similar, masked_floor)
            best = jnp.max(similar, axis=1, keepdims=True)
            best_all = jnp.where(lane == s, best, best_all)
        score[pl.ds(b, 1), :] = jnp.sum(best_all, axis=0, keepdims=True) * (1.0 / full_tokens)
        return 0

    lax.fori_loop(0, blocks, block, 0)
    for b in range(blocks):
        r = slice(b * queries, (b + 1) * queries)
        line = jnp.broadcast_to(score[b : b + 1, :], (queries, width))
        line = jnp.take_along_axis(line, rank[r], axis=1)
        out_ref[r, :] = jnp.where(here[r], line, 0.0)


def whole(n, *spaces):
    return [pl.BlockSpec(memory_space=s) for s in spaces] * n


def body(queries, candidates, residuals, centroid_ids, block_scales, lengths, centroids, bucket_weights):
    shards = lax.axis_size("shard")
    halves = lax.axis_size("sub")
    query_count, picks = candidates.shape
    tokens, width = queries.shape[1:]
    passages, slots, words = residuals.shape
    capacity = max(2, 2 * query_count * picks // (shards * halves))
    me = (lax.axis_index("shard") * halves + lax.axis_index("sub")).reshape(1)

    def swap_shard(x, d):
        return lax.ppermute(x, "shard", [(i, i ^ d) for i in range(shards)])

    def swap_sub(x):
        return lax.ppermute(x, "sub", [(i, i ^ 1) for i in range(halves)])

    payload = pl.pallas_call(
        functools.partial(pack_kernel, words, passages),
        out_shape=jax.ShapeDtypeStruct((query_count * (tokens + 2), width), jnp.bfloat16),
        in_specs=whole(2, VMEM),
        out_specs=pl.BlockSpec(memory_space=VMEM),
        compiler_params=LIMIT,
        name="pack",
    )(queries, candidates)

    embedded = pl.pallas_call(
        decode_kernel,
        out_shape=jax.ShapeDtypeStruct((passages, width, slots), jnp.bfloat16),
        in_specs=whole(2, SMEM) + whole(4, VMEM),
        out_specs=pl.BlockSpec(memory_space=VMEM),
        scratch_shapes=[
            VMEM((centroids.shape[0], width), jnp.float32),
            VMEM((2, slots, width), jnp.bfloat16),
        ],
        compiler_params=LIMIT,
        name="decode",
    )(
        centroid_ids,
        lengths,
        jnp.swapaxes(residuals, 1, 2),
        block_scales.astype(jnp.float32),
        centroids,
        bucket_weights.reshape(1, 4),
    )

    def score(mine, other):
        blocks = mine.shape[0]
        padded = -(-blocks // 8) * 8
        return pl.pallas_call(
            functools.partial(pair_kernel, query_count, picks, capacity),
            out_shape=jax.ShapeDtypeStruct((blocks * query_count, width), jnp.float32),
            in_specs=whole(2, SMEM) + whole(3, VMEM),
            out_specs=pl.BlockSpec(memory_space=VMEM),
            scratch_shapes=[
                VMEM((2 * padded, width), jnp.int32),
                SMEM((2 * padded, width), jnp.int32),
                VMEM((padded, width), jnp.float32),
                pltpu.SemaphoreType.DMA,
            ],
            compiler_params=LIMIT,
            name="pairs",
        )(me, lengths, mine, other, embedded)

    held = payload[None]
    steps = []
    d = shards // 2
    while d > 1:
        held = jnp.concatenate([held, swap_shard(held, d)], axis=0)
        steps.append(d)
        d //= 2
    far = swap_shard(held, 1)
    near_scores = score(held, swap_sub(held))
    far_scores = score(far, swap_sub(far))
    total = near_scores[:, :picks] + swap_shard(far_scores[:, :picks], 1)
    for d in reversed(steps):
        half = total.shape[0] // 2
        total = total[:half] + swap_shard(total[half:], d)
    return total + swap_sub(total)


def solution(mesh):
    return jax.shard_map(
        body,
        mesh=mesh,
        in_specs=(
            P(("groups", "shard"), "sub", None),
            P(("groups", "shard"), None),
            P(("shard", "sub"), None, None),
            P(("shard", "sub"), None),
            P(("shard", "sub"), None),
            P(("shard", "sub")),
            P(),
            P(),
        ),
        out_specs=P(("groups", "shard"), None),
        check_vma=False,
    )
```

```python
import functools

import jax
import jax.numpy as jnp
from jax import lax
from jax.experimental import pallas as pl
from jax.experimental.pallas import tpu as pltpu
from jax.sharding import PartitionSpec as P

masked_floor = -1000000000.0
VMEM = pltpu.VMEM
SMEM = pltpu.SMEM
LIMIT = pltpu.CompilerParams(vmem_limit_bytes=40 * 2**20)


def iota(shape, dim):
    return lax.broadcasted_iota(jnp.int32, shape, dim)


def ones_where(mask):
    return jnp.where(mask, 1.0, 0.0).astype(jnp.bfloat16)


def dot(a, b, contract=((1,), (0,))):
    return lax.dot_general(a, b, (contract, ((), ())), preferred_element_type=jnp.float32)


def spread(feature, words, per):
    return per * (feature % words) + feature // words


def pack_kernel(words, passages, query_hbm, cand_hbm, out_ref, query_ref, cand_ref, sems):
    copies = [
        pltpu.make_async_copy(query_hbm, query_ref, sems.at[0]),
        pltpu.make_async_copy(cand_hbm, cand_ref, sems.at[1]),
    ]
    for c in copies:
        c.start()
    count, tokens, width = query_ref.shape
    per = width // words
    order = ones_where(iota((width, width), 0) == spread(iota((width, width), 1), words, per))
    picks = cand_ref.shape[1]
    repeat = ones_where(iota((picks, width), 0) == iota((picks, width), 1) % picks)
    for c in copies:
        c.wait()
    flat = query_ref[...].reshape(count * tokens, width)
    rows = count * tokens
    out_ref[0:rows, :] = dot(flat, order).astype(jnp.bfloat16)
    ids = cand_ref[...]
    owner = ids // passages
    local = ids - owner * passages
    for i, part in enumerate((owner, local)):
        part = part.astype(jnp.float32).astype(jnp.bfloat16)
        out_ref[rows + i * count : rows + (i + 1) * count, :] = dot(part, repeat).astype(jnp.bfloat16)


WIDE = 4


def decode_kernel(first, start, stop, *refs):
    if first:
        ids_hbm, words_hbm, scale_hbm, bucket_hbm, table_hbm, out_ref, wide = refs[:7]
        rest = refs[7:]
    else:
        ids_hbm, words_hbm, scale_hbm, bucket_hbm, wide, _, out_ref = refs[:7]
        rest = refs[7:]
    rows, ids_ref, words_ref, scale_bf, scale_ref, bucket_ref, sems = rest[:7]
    mine = pl.ds(start, stop - start)
    copies = [
        pltpu.make_async_copy(ids_hbm.at[mine], ids_ref, sems.at[0]),
        pltpu.make_async_copy(words_hbm.at[mine], words_ref, sems.at[1]),
        pltpu.make_async_copy(scale_hbm, scale_bf, sems.at[2]),
        pltpu.make_async_copy(bucket_hbm, bucket_ref, sems.at[3]),
    ]
    if first:
        table_ref = rest[7]
        parts = 4
        size = table_ref.shape[0] // parts
        loads = [
            pltpu.make_async_copy(
                table_hbm.at[pl.ds(i * size, size)], table_ref.at[pl.ds(i * size, size)], sems.at[4 + i]
            )
            for i in range(parts)
        ]
        for c in loads + copies:
            c.start()
        chunk = 256
        for i in range(parts):
            loads[i].wait()

            def widen(j, _):
                r = pl.ds(pl.multiple_of(i * size + j * chunk, chunk), chunk)
                wide[r, :] = table_ref[r, :].astype(jnp.float32)
                return 0

            lax.fori_loop(0, size // chunk, widen, 0)
    else:
        for c in copies:
            c.start()
    for c in copies:
        c.wait()
    scale_ref[...] = scale_bf[...].astype(jnp.float32)
    slots = ids_ref.shape[1]
    width = wide.shape[1]
    words = words_ref.shape[1]
    per = width // words
    order = ones_where(iota((width, width), 1) == spread(iota((width, width), 0), words, per))
    levels = [
        jnp.broadcast_to(bucket_ref[0:1, i : i + 1].astype(jnp.float32), (words, slots * WIDE))
        for i in range(4)
    ]

    def fetch(p, buf):
        for u in range(WIDE):
            for g in range(slots // 16):
                got = jnp.concatenate(
                    [wide[pl.ds(ids_ref[p + u, g * 16 + i], 1), :] for i in range(16)], axis=0
                )
                r = u * slots + g * 16
                rows[buf, r : r + 16, :] = got.astype(jnp.bfloat16)
                yield

    def build(p, buf, fetching):
        packed = jnp.concatenate([words_ref[p + u] for u in range(WIDE)], axis=1)
        centre = dot(order, rows[buf], ((1,), (1,)))
        parts = []
        for k in range(per):
            for _ in range(WIDE):
                next(fetching, None)
            low = (packed & (1 << (2 * k))) != 0
            high = (packed & (2 << (2 * k))) != 0
            parts.append(
                jnp.where(
                    high,
                    jnp.where(low, levels[3], levels[2]),
                    jnp.where(low, levels[1], levels[0]),
                )
            )
        value = jnp.concatenate(parts, axis=0)
        scale = jnp.concatenate([scale_ref[pl.ds(start + p + u, 1), :] for u in range(WIDE)], axis=1)
        raw = centre + scale * value
        inverse = lax.rsqrt(jnp.sum(raw * raw, axis=0, keepdims=True) + 1e-06)
        out = (raw * inverse).astype(jnp.bfloat16)
        for u in range(WIDE):
            out_ref[start + p + u] = out[:, u * slots : (u + 1) * slots]
        for _ in fetching:
            pass

    for _ in fetch(0, 0):
        pass

    def step(i, _):
        p = 2 * WIDE * i
        build(p, 0, fetch(p + WIDE, 1))
        build(p + WIDE, 1, fetch(p + 2 * WIDE, 0))
        return 0

    last = stop - start - 2 * WIDE
    lax.fori_loop(0, last // (2 * WIDE), step, 0)
    build(last, 0, fetch(last + WIDE, 1))
    build(last + WIDE, 1, iter(()))


def slot_kernel(queries, picks, capacity, rows_ref, slot_ref, rank_ref):
    blocks = rows_ref.shape[0]
    width = rows_ref.shape[2]
    body_rows = rows_ref.shape[1] - 2 * queries
    groups = width // picks
    rows = blocks * queries
    me = lax.axis_index("shard") * lax.axis_size("sub") + lax.axis_index("sub")
    owner = rows_ref[:, body_rows : body_rows + queries, :].reshape(rows, width).astype(jnp.float32)
    local = (
        rows_ref[:, body_rows + queries : body_rows + 2 * queries, :]
        .reshape(rows, width)
        .astype(jnp.float32)
    )
    here = owner == jnp.full((rows, width), me, jnp.int32).astype(jnp.float32)
    here_bf = ones_where(here)
    li = iota((width, width), 0)
    lj = iota((width, width), 1)
    before_lane = ones_where((li < picks) & (li < lj % picks))
    whole_row = ones_where(li < picks)
    ri = iota((rows, rows), 0)
    rj = iota((rows, rows), 1)
    before_row = ones_where((ri // queries == rj // queries) & (rj < ri))
    totals = dot(here_bf, whole_row).astype(jnp.bfloat16)
    rank = dot(here_bf, before_lane) + dot(before_row, totals)
    rank = rank.astype(jnp.int32)
    rank_ref[...] = jnp.where(here, rank, -1)
    lane_group = iota((rows, width), 1) // picks
    which = (iota((rows, width), 0) % queries).astype(jnp.float32)
    padded = slot_ref.shape[0] // 2
    collect = ones_where(iota((padded, rows), 0) == iota((padded, rows), 1) // queries)
    slot_q = jnp.zeros((padded, width), jnp.float32)
    slot_p = jnp.zeros((padded, width), jnp.float32)
    for i in range(-(-capacity // groups)):
        chosen = here & (rank == i * groups + lane_group)
        to_slot = ones_where(lj == i * groups + li // picks)
        got_q = dot(collect, jnp.where(chosen, which, 0.0).astype(jnp.bfloat16))
        got_p = dot(collect, jnp.where(chosen, local, 0.0).astype(jnp.bfloat16))
        slot_q += dot(got_q.astype(jnp.bfloat16), to_slot)
        slot_p += dot(got_p.astype(jnp.bfloat16), to_slot)
    slot_ref[0:padded, :] = slot_q.astype(jnp.int32)
    slot_ref[padded : 2 * padded, :] = slot_p.astype(jnp.int32)


def pair_kernel(
    queries, picks, capacity, len_hbm, slot_ref, rank_ref, mine_ref, other_ref, emb_ref, out_ref, slot_s, len_s, score, sems
):
    copies = [
        pltpu.make_async_copy(slot_ref, slot_s, sems.at[0]),
        pltpu.make_async_copy(len_hbm, len_s, sems.at[1]),
    ]
    for c in copies:
        c.start()
    for c in copies:
        c.wait()
    blocks = mine_ref.shape[0]
    width = mine_ref.shape[2]
    tokens = (mine_ref.shape[1] - 2 * queries) // queries
    padded = slot_s.shape[0] // 2
    full_tokens = 2 * tokens
    lane = iota((full_tokens, width), 1)

    def block(b, _):
        best_all = jnp.zeros((full_tokens, width), jnp.float32)
        for s in range(capacity):
            p = slot_s[padded + b, s]
            r = pl.ds(pl.multiple_of(slot_s[b, s] * tokens, tokens), tokens)
            rows_q = jnp.concatenate([mine_ref[b, r, :], other_ref[b, r, :]], axis=0)
            similar = dot(rows_q, emb_ref[p])
            similar = jnp.where(lane < len_s[p], similar, masked_floor)
            best = jnp.max(similar, axis=1, keepdims=True)
            best_all = jnp.where(lane == s, best, best_all)
        score[pl.ds(b, 1), :] = jnp.sum(best_all, axis=0, keepdims=True) * (1.0 / full_tokens)
        return 0

    lax.fori_loop(0, blocks, block, 0)
    groups = width // picks
    lane_group = iota((queries, width), 1) // picks
    for c in range(0, blocks, groups):
        out = jnp.zeros((queries, width), jnp.float32)
        for b in range(c, min(c + groups, blocks)):
            rank = rank_ref[b * queries : (b + 1) * queries, :]
            line = jnp.broadcast_to(score[b : b + 1, :], (queries, width))
            line = jnp.take_along_axis(line, jnp.maximum(rank, 0), axis=1)
            out = jnp.where((rank >= 0) & (lane_group == b - c), line, out)
        out_ref[:, c * picks : c * picks + width] = out


def whole(n, *spaces):
    return [pl.BlockSpec(memory_space=s) for s in spaces] * n


def body(queries, candidates, residuals, centroid_ids, block_scales, lengths, centroids, bucket_weights):
    shards = lax.axis_size("shard")
    halves = lax.axis_size("sub")
    query_count, picks = candidates.shape
    tokens, width = queries.shape[1:]
    passages, slots, words = residuals.shape
    capacity = max(2, 2 * query_count * picks // (shards * halves))

    def swap_shard(x, d):
        return lax.ppermute(x, "shard", [(i, i ^ d) for i in range(shards)])

    def swap_sub(x):
        return lax.ppermute(x, "sub", [(i, i ^ 1) for i in range(halves)])

    payload = pl.pallas_call(
        functools.partial(pack_kernel, words, passages),
        out_shape=jax.ShapeDtypeStruct((query_count * (tokens + 2), width), jnp.bfloat16),
        in_specs=whole(2, pltpu.HBM),
        out_specs=pl.BlockSpec(memory_space=VMEM),
        scratch_shapes=[
            VMEM(queries.shape, queries.dtype),
            VMEM(candidates.shape, candidates.dtype),
            pltpu.SemaphoreType.DMA((2,)),
        ],
        compiler_params=LIMIT,
        name="pack",
    )(queries, candidates)

    stored = (
        centroid_ids,
        jnp.swapaxes(residuals, 1, 2),
        block_scales,
        bucket_weights.reshape(1, 4),
    )
    emb_shape = jax.ShapeDtypeStruct((passages, width, slots), jnp.bfloat16)
    wide_shape = jax.ShapeDtypeStruct(centroids.shape, jnp.float32)

    def decode(start, stop, wide, embedded):
        first = embedded is None
        extra = (centroids,) if first else (wide, embedded)
        return pl.pallas_call(
            functools.partial(decode_kernel, first, start, stop),
            out_shape=(emb_shape, wide_shape) if first else emb_shape,
            in_specs=whole(5, pltpu.HBM) if first else whole(4, pltpu.HBM) + whole(2, VMEM),
            out_specs=(pl.BlockSpec(memory_space=VMEM),) * 2 if first else pl.BlockSpec(memory_space=VMEM),
            scratch_shapes=[
                VMEM((2, WIDE * slots, width), jnp.bfloat16),
                SMEM((stop - start, slots), jnp.int32),
                VMEM((stop - start, words, slots), jnp.int32),
                VMEM(block_scales.shape, block_scales.dtype),
                VMEM(block_scales.shape, jnp.float32),
                VMEM((1, 4), bucket_weights.dtype),
                pltpu.SemaphoreType.DMA((8 if first else 4,)),
            ]
            + ([VMEM(centroids.shape, centroids.dtype)] if first else []),
            input_output_aliases={} if first else {5: 0},
            compiler_params=LIMIT,
            cost_estimate=pl.CostEstimate(
                flops=(stop - start) * 2 * 10**8, bytes_accessed=0, transcendentals=0
            ),
            name="decode",
        )(*stored, *extra)

    def find(mine):
        blocks = mine.shape[0]
        padded = -(-blocks // 8) * 8
        return pl.pallas_call(
            functools.partial(slot_kernel, query_count, picks, capacity),
            out_shape=(
                jax.ShapeDtypeStruct((2 * padded, width), jnp.int32),
                jax.ShapeDtypeStruct((blocks * query_count, width), jnp.int32),
            ),
            in_specs=whole(1, VMEM),
            out_specs=(pl.BlockSpec(memory_space=VMEM),) * 2,
            compiler_params=LIMIT,
            cost_estimate=pl.CostEstimate(flops=10**9, bytes_accessed=0, transcendentals=0),
            name="slots",
        )(mine)

    def score(found, mine, other):
        blocks = mine.shape[0]
        padded = -(-blocks // 8) * 8
        lanes = -(-blocks * picks // width) * width
        return pl.pallas_call(
            functools.partial(pair_kernel, query_count, picks, capacity),
            out_shape=jax.ShapeDtypeStruct((query_count, lanes), jnp.float32),
            in_specs=whole(1, pltpu.HBM) + whole(5, VMEM),
            out_specs=pl.BlockSpec(memory_space=VMEM),
            scratch_shapes=[
                SMEM((2 * padded, width), jnp.int32),
                SMEM(lengths.shape, jnp.int32),
                VMEM((padded, width), jnp.float32),
                pltpu.SemaphoreType.DMA((2,)),
            ],
            compiler_params=LIMIT,
            cost_estimate=pl.CostEstimate(flops=3 * 10**9, bytes_accessed=0, transcendentals=0),
            name="pairs",
        )(lengths, *found, mine, other, embedded)[:, : blocks * picks]

    steps = []
    d = shards // 2
    while d >= 1:
        steps.append(d)
        d //= 2
    unit = 2 * WIDE
    cuts = [passages // unit * i // len(steps) * unit for i in range(len(steps) + 1)]
    held = payload[None]
    wide = embedded = None
    for i, d in enumerate(steps):
        moved = swap_shard(held, d)
        if cuts[i] < cuts[i + 1]:
            if embedded is None:
                embedded, wide = decode(cuts[i], cuts[i + 1], None, None)
            else:
                embedded = decode(cuts[i], cuts[i + 1], wide, embedded)
        if d > 1:
            moved, embedded = lax.optimization_barrier((moved, embedded))
            held = jnp.concatenate([held, moved], axis=0)
        else:
            far = moved
    near_scores = score(find(held), held, swap_sub(held))
    far, near_scores = lax.optimization_barrier((far, near_scores))
    far_scores = score(find(far), far, swap_sub(far))
    total = near_scores + swap_shard(far_scores, 1)
    for d in reversed(steps[:-1]):
        half = total.shape[1] // 2
        total = total[:, :half] + swap_shard(total[:, half:], d)
    return total + swap_sub(total)


def solution(mesh):
    return jax.shard_map(
        body,
        mesh=mesh,
        in_specs=(
            P(("groups", "shard"), "sub", None),
            P(("groups", "shard"), None),
            P(("shard", "sub"), None, None),
            P(("shard", "sub"), None),
            P(("shard", "sub"), None),
            P(("shard", "sub")),
            P(),
            P(),
        ),
        out_specs=P(("groups", "shard"), None),
        check_vma=False,
    )
```

```python
import functools

import jax
import jax.numpy as jnp
from jax import lax
from jax.experimental import pallas as pl
from jax.experimental.pallas import tpu as pltpu
from jax.sharding import PartitionSpec as P

masked_floor = -1000000000.0
VMEM = pltpu.VMEM
SMEM = pltpu.SMEM
LIMIT = pltpu.CompilerParams(vmem_limit_bytes=40 * 2**20)


def iota(shape, dim):
    return lax.broadcasted_iota(jnp.int32, shape, dim)


def ones_where(mask):
    return jnp.where(mask, 1.0, 0.0).astype(jnp.bfloat16)


def dot(a, b, contract=((1,), (0,))):
    return lax.dot_general(a, b, (contract, ((), ())), preferred_element_type=jnp.float32)


def spread(feature, words, per):
    return per * (feature % words) + feature // words


def pack_kernel(words, passages, query_hbm, cand_hbm, out_ref, query_ref, cand_ref, sems):
    copies = [
        pltpu.make_async_copy(query_hbm, query_ref, sems.at[0]),
        pltpu.make_async_copy(cand_hbm, cand_ref, sems.at[1]),
    ]
    for c in copies:
        c.start()
    count, tokens, width = query_ref.shape
    per = width // words
    order = ones_where(iota((width, width), 0) == spread(iota((width, width), 1), words, per))
    picks = cand_ref.shape[1]
    repeat = ones_where(iota((picks, width), 0) == iota((picks, width), 1) % picks)
    for c in copies:
        c.wait()
    flat = query_ref[...].reshape(count * tokens, width)
    rows = count * tokens
    out_ref[0:rows, :] = dot(flat, order).astype(jnp.bfloat16)
    ids = cand_ref[...]
    owner = ids // passages
    local = ids - owner * passages
    for i, part in enumerate((owner, local)):
        part = part.astype(jnp.float32).astype(jnp.bfloat16)
        out_ref[rows + i * count : rows + (i + 1) * count, :] = dot(part, repeat).astype(jnp.bfloat16)


WIDE = 4


def decode_kernel(first, start, stop, *refs):
    if first:
        ids_hbm, words_hbm, scale_hbm, bucket_hbm, table_hbm, out_ref, wide = refs[:7]
        rest = refs[7:]
    else:
        ids_hbm, words_hbm, scale_hbm, bucket_hbm, wide, _, out_ref = refs[:7]
        rest = refs[7:]
    rows, ids_ref, words_ref, scale_bf, scale_ref, bucket_ref, sems = rest[:7]
    mine = pl.ds(start, stop - start)
    copies = [
        pltpu.make_async_copy(ids_hbm.at[mine], ids_ref, sems.at[0]),
        pltpu.make_async_copy(words_hbm.at[mine], words_ref, sems.at[1]),
        pltpu.make_async_copy(scale_hbm, scale_bf, sems.at[2]),
        pltpu.make_async_copy(bucket_hbm, bucket_ref, sems.at[3]),
    ]
    if first:
        table_ref = rest[7]
        parts = 4
        size = table_ref.shape[0] // parts
        loads = [
            pltpu.make_async_copy(
                table_hbm.at[pl.ds(i * size, size)], table_ref.at[pl.ds(i * size, size)], sems.at[4 + i]
            )
            for i in range(parts)
        ]
        for c in loads + copies:
            c.start()
        chunk = 256
        for i in range(parts):
            loads[i].wait()

            def widen(j, _):
                r = pl.ds(pl.multiple_of(i * size + j * chunk, chunk), chunk)
                wide[r, :] = table_ref[r, :].astype(jnp.float32)
                return 0

            lax.fori_loop(0, size // chunk, widen, 0)
    else:
        for c in copies:
            c.start()
    for c in copies:
        c.wait()
    scale_ref[...] = scale_bf[...].astype(jnp.float32)
    slots = ids_ref.shape[1]
    width = wide.shape[1]
    words = words_ref.shape[1]
    per = width // words
    order = ones_where(iota((width, width), 1) == spread(iota((width, width), 0), words, per))
    levels = [
        jnp.broadcast_to(bucket_ref[0:1, i : i + 1].astype(jnp.float32), (words, slots * WIDE))
        for i in range(4)
    ]

    def fetch(p, buf):
        for u in range(WIDE):
            for g in range(slots // 16):
                got = jnp.concatenate(
                    [wide[pl.ds(ids_ref[p + u, g * 16 + i], 1), :] for i in range(16)], axis=0
                )
                r = u * slots + g * 16
                rows[buf, r : r + 16, :] = got.astype(jnp.bfloat16)
                yield

    def build(p, buf, fetching):
        packed = jnp.concatenate([words_ref[p + u] for u in range(WIDE)], axis=1)
        centre = dot(order, rows[buf], ((1,), (1,)))
        parts = []
        for k in range(per):
            for _ in range(WIDE):
                next(fetching, None)
            low = (packed & (1 << (2 * k))) != 0
            high = (packed & (2 << (2 * k))) != 0
            parts.append(
                jnp.where(
                    high,
                    jnp.where(low, levels[3], levels[2]),
                    jnp.where(low, levels[1], levels[0]),
                )
            )
        value = jnp.concatenate(parts, axis=0)
        scale = jnp.concatenate([scale_ref[pl.ds(start + p + u, 1), :] for u in range(WIDE)], axis=1)
        raw = centre + scale * value
        inverse = lax.rsqrt(jnp.sum(raw * raw, axis=0, keepdims=True) + 1e-06)
        out = (raw * inverse).astype(jnp.bfloat16)
        for u in range(WIDE):
            out_ref[start + p + u] = out[:, u * slots : (u + 1) * slots]
        for _ in fetching:
            pass

    for _ in fetch(0, 0):
        pass

    def step(i, _):
        p = 2 * WIDE * i
        build(p, 0, fetch(p + WIDE, 1))
        build(p + WIDE, 1, fetch(p + 2 * WIDE, 0))
        return 0

    last = stop - start - 2 * WIDE
    for i in range(last // (2 * WIDE)):
        step(i, 0)
    build(last, 0, fetch(last + WIDE, 1))
    build(last + WIDE, 1, iter(()))


def slot_kernel(queries, picks, capacity, rows_ref, slot_ref, rank_ref):
    blocks = rows_ref.shape[0]
    width = rows_ref.shape[2]
    body_rows = rows_ref.shape[1] - 2 * queries
    groups = width // picks
    rows = blocks * queries
    me = lax.axis_index("shard") * lax.axis_size("sub") + lax.axis_index("sub")
    owner = rows_ref[:, body_rows : body_rows + queries, :].reshape(rows, width).astype(jnp.float32)
    local = (
        rows_ref[:, body_rows + queries : body_rows + 2 * queries, :]
        .reshape(rows, width)
        .astype(jnp.float32)
    )
    here = owner == jnp.full((rows, width), me, jnp.int32).astype(jnp.float32)
    here_bf = ones_where(here)
    li = iota((width, width), 0)
    lj = iota((width, width), 1)
    before_lane = ones_where((li < picks) & (li < lj % picks))
    whole_row = ones_where(li < picks)
    ri = iota((rows, rows), 0)
    rj = iota((rows, rows), 1)
    before_row = ones_where((ri // queries == rj // queries) & (rj < ri))
    totals = dot(here_bf, whole_row).astype(jnp.bfloat16)
    rank = dot(here_bf, before_lane) + dot(before_row, totals)
    rank = rank.astype(jnp.int32)
    rank_ref[...] = jnp.where(here, rank, -1)
    lane_group = iota((rows, width), 1) // picks
    which = (iota((rows, width), 0) % queries).astype(jnp.float32)
    padded = slot_ref.shape[0] // 2
    collect = ones_where(iota((padded, rows), 0) == iota((padded, rows), 1) // queries)
    slot_q = jnp.zeros((padded, width), jnp.float32)
    slot_p = jnp.zeros((padded, width), jnp.float32)
    for i in range(-(-capacity // groups)):
        chosen = here & (rank == i * groups + lane_group)
        to_slot = ones_where(lj == i * groups + li // picks)
        got_q = dot(collect, jnp.where(chosen, which, 0.0).astype(jnp.bfloat16))
        got_p = dot(collect, jnp.where(chosen, local, 0.0).astype(jnp.bfloat16))
        slot_q += dot(got_q.astype(jnp.bfloat16), to_slot)
        slot_p += dot(got_p.astype(jnp.bfloat16), to_slot)
    slot_ref[0:padded, :] = slot_q.astype(jnp.int32)
    slot_ref[padded : 2 * padded, :] = slot_p.astype(jnp.int32)


def pair_kernel(
    queries, picks, capacity, len_hbm, slot_ref, rank_ref, mine_ref, other_ref, emb_ref, out_ref, slot_s, len_s, score, sems
):
    copies = [
        pltpu.make_async_copy(slot_ref, slot_s, sems.at[0]),
        pltpu.make_async_copy(len_hbm, len_s, sems.at[1]),
    ]
    for c in copies:
        c.start()
    for c in copies:
        c.wait()
    blocks = mine_ref.shape[0]
    width = mine_ref.shape[2]
    tokens = (mine_ref.shape[1] - 2 * queries) // queries
    padded = slot_s.shape[0] // 2
    full_tokens = 2 * tokens
    slots = emb_ref.shape[2]
    lane = iota((full_tokens, slots), 1)
    spot = iota((full_tokens, width), 1)

    def block(b, _):
        best_all = jnp.zeros((full_tokens, width), jnp.float32)
        for s in range(0, capacity, 2):
            asked = []
            kept = []
            stored = []
            for j in range(s, s + 2):
                p = slot_s[padded + b, j]
                r = pl.ds(pl.multiple_of(slot_s[b, j] * tokens, tokens), tokens)
                asked += [mine_ref[b, r, :], other_ref[b, r, :]]
                stored.append(emb_ref[p])
                kept.append(len_s[p])
            both = dot(jnp.concatenate(asked, axis=0), jnp.concatenate(stored, axis=1))
            for j in range(2):
                similar = both[j * full_tokens : (j + 1) * full_tokens, j * slots : (j + 1) * slots]
                similar = jnp.where(lane < kept[j], similar, masked_floor)
                best = jnp.max(similar, axis=1, keepdims=True)
                best_all = jnp.where(spot == s + j, best, best_all)
        score[pl.ds(b, 1), :] = jnp.sum(best_all, axis=0, keepdims=True) * (1.0 / full_tokens)
        return 0

    lax.fori_loop(0, blocks, block, 0)
    groups = width // picks
    lane_group = iota((queries, width), 1) // picks
    for c in range(0, blocks, groups):
        out = jnp.zeros((queries, width), jnp.float32)
        for b in range(c, min(c + groups, blocks)):
            rank = rank_ref[b * queries : (b + 1) * queries, :]
            line = jnp.broadcast_to(score[b : b + 1, :], (queries, width))
            line = jnp.take_along_axis(line, jnp.maximum(rank, 0), axis=1)
            out = jnp.where((rank >= 0) & (lane_group == b - c), line, out)
        out_ref[:, c * picks : c * picks + width] = out


def whole(n, *spaces):
    return [pl.BlockSpec(memory_space=s) for s in spaces] * n


def body(queries, candidates, residuals, centroid_ids, block_scales, lengths, centroids, bucket_weights):
    shards = lax.axis_size("shard")
    halves = lax.axis_size("sub")
    query_count, picks = candidates.shape
    tokens, width = queries.shape[1:]
    passages, slots, words = residuals.shape
    capacity = max(2, 2 * query_count * picks // (shards * halves))

    def swap_shard(x, d):
        return lax.ppermute(x, "shard", [(i, i ^ d) for i in range(shards)])

    def swap_sub(x):
        return lax.ppermute(x, "sub", [(i, i ^ 1) for i in range(halves)])

    payload = pl.pallas_call(
        functools.partial(pack_kernel, words, passages),
        out_shape=jax.ShapeDtypeStruct((query_count * (tokens + 2), width), jnp.bfloat16),
        in_specs=whole(2, pltpu.HBM),
        out_specs=pl.BlockSpec(memory_space=VMEM),
        scratch_shapes=[
            VMEM(queries.shape, queries.dtype),
            VMEM(candidates.shape, candidates.dtype),
            pltpu.SemaphoreType.DMA((2,)),
        ],
        compiler_params=LIMIT,
        cost_estimate=pl.CostEstimate(flops=6 * 10**9, bytes_accessed=0, transcendentals=0),
        name="pack",
    )(queries, candidates)

    stored = (
        centroid_ids,
        jnp.swapaxes(residuals, 1, 2),
        block_scales,
        bucket_weights.reshape(1, 4),
    )
    emb_shape = jax.ShapeDtypeStruct((passages, width, slots), jnp.bfloat16)
    wide_shape = jax.ShapeDtypeStruct(centroids.shape, jnp.float32)

    def decode(start, stop, wide, embedded):
        if start == stop:
            return embedded, wide
        first = embedded is None
        extra = (centroids,) if first else (wide, embedded)
        out = pl.pallas_call(
            functools.partial(decode_kernel, first, start, stop),
            out_shape=(emb_shape, wide_shape) if first else emb_shape,
            in_specs=whole(5, pltpu.HBM) if first else whole(4, pltpu.HBM) + whole(2, VMEM),
            out_specs=(pl.BlockSpec(memory_space=VMEM),) * 2 if first else pl.BlockSpec(memory_space=VMEM),
            scratch_shapes=[
                VMEM((2, WIDE * slots, width), jnp.bfloat16),
                SMEM((stop - start, slots), jnp.int32),
                VMEM((stop - start, words, slots), jnp.int32),
                VMEM(block_scales.shape, block_scales.dtype),
                VMEM(block_scales.shape, jnp.float32),
                VMEM((1, 4), bucket_weights.dtype),
                pltpu.SemaphoreType.DMA((8 if first else 4,)),
            ]
            + ([VMEM(centroids.shape, centroids.dtype)] if first else []),
            input_output_aliases={} if first else {5: 0},
            compiler_params=LIMIT,
            cost_estimate=pl.CostEstimate(
                flops=(stop - start) * 2 * 10**8, bytes_accessed=0, transcendentals=0
            ),
            name="decode",
        )(*stored, *extra)
        return out if first else (out, wide)

    def find(mine):
        blocks = mine.shape[0]
        padded = -(-blocks // 8) * 8
        return pl.pallas_call(
            functools.partial(slot_kernel, query_count, picks, capacity),
            out_shape=(
                jax.ShapeDtypeStruct((2 * padded, width), jnp.int32),
                jax.ShapeDtypeStruct((blocks * query_count, width), jnp.int32),
            ),
            in_specs=whole(1, VMEM),
            out_specs=(pl.BlockSpec(memory_space=VMEM),) * 2,
            compiler_params=LIMIT,
            cost_estimate=pl.CostEstimate(flops=10**9, bytes_accessed=0, transcendentals=0),
            name="slots",
        )(mine)

    def score(found, mine, other):
        blocks = mine.shape[0]
        padded = -(-blocks // 8) * 8
        lanes = -(-blocks * picks // width) * width
        return pl.pallas_call(
            functools.partial(pair_kernel, query_count, picks, capacity),
            out_shape=jax.ShapeDtypeStruct((query_count, lanes), jnp.float32),
            in_specs=whole(1, pltpu.HBM) + whole(5, VMEM),
            out_specs=pl.BlockSpec(memory_space=VMEM),
            scratch_shapes=[
                SMEM((2 * padded, width), jnp.int32),
                SMEM(lengths.shape, jnp.int32),
                VMEM((padded, width), jnp.float32),
                pltpu.SemaphoreType.DMA((2,)),
            ],
            compiler_params=LIMIT,
            cost_estimate=pl.CostEstimate(flops=3 * 10**9, bytes_accessed=0, transcendentals=0),
            name="pairs",
        )(lengths, *found, mine, other, embedded)[:, : blocks * picks]

    steps = []
    d = shards // 2
    while d >= 1:
        steps.append(d)
        d //= 2
    unit = 2 * WIDE
    units = passages // unit
    parts = len(steps)
    cuts = [-(-units * i // parts) * unit for i in range(parts + 1)]
    held = payload[None]
    wide = embedded = None
    for i, d in enumerate(steps[:-2]):
        moved = swap_shard(held, d)
        embedded, wide = decode(cuts[i], cuts[i + 1], wide, embedded)
        moved, embedded = lax.optimization_barrier((moved, embedded))
        held = jnp.concatenate([held, moved], axis=0)
    moved = swap_shard(held, steps[-2])
    far_a = swap_shard(held, 1)
    embedded, wide = decode(cuts[-3], cuts[-2], wide, embedded)
    moved, embedded = lax.optimization_barrier((moved, embedded))
    far_b = swap_shard(moved, 1)
    embedded, wide = decode(cuts[-2], cuts[-1], wide, embedded)
    near = jnp.concatenate([held, moved], axis=0)
    near_scores = score(find(near), near, swap_sub(near))
    far_b, near_scores = lax.optimization_barrier((far_b, near_scores))
    far = jnp.concatenate([far_a, far_b], axis=0)
    far_scores = score(find(far), far, swap_sub(far))
    total = near_scores + swap_shard(far_scores, 1)
    for d in reversed(steps[:-1]):
        half = total.shape[1] // 2
        total = total[:, :half] + swap_shard(total[:, half:], d)
    return total + swap_sub(total)


def solution(mesh):
    return jax.shard_map(
        body,
        mesh=mesh,
        in_specs=(
            P(("groups", "shard"), "sub", None),
            P(("groups", "shard"), None),
            P(("shard", "sub"), None, None),
            P(("shard", "sub"), None),
            P(("shard", "sub"), None),
            P(("shard", "sub")),
            P(),
            P(),
        ),
        out_specs=P(("groups", "shard"), None),
        check_vma=False,
    )
```

```python
import functools
import math

import jax
import jax.numpy as jnp
from jax import lax
from jax.experimental import pallas as pl
from jax.experimental.pallas import tpu as pltpu
from jax.sharding import PartitionSpec as P

masked_floor = -1000000000.0
UNROLLED = 128
VMEM = pltpu.VMEM
SMEM = pltpu.SMEM
LIMIT = pltpu.CompilerParams(vmem_limit_bytes=40 * 2**20)


def iota(shape, dim):
    return lax.broadcasted_iota(jnp.int32, shape, dim)


def ones_where(mask):
    return jnp.where(mask, 1.0, 0.0).astype(jnp.bfloat16)


def dot(a, b, contract=((1,), (0,))):
    return lax.dot_general(a, b, (contract, ((), ())), preferred_element_type=jnp.float32)


def spread(feature, words, per):
    return per * (feature % words) + feature // words


def pack_kernel(words, passages, query_hbm, cand_hbm, out_ref, query_ref, cand_ref, sems):
    copies = [
        pltpu.make_async_copy(query_hbm, query_ref, sems.at[0]),
        pltpu.make_async_copy(cand_hbm, cand_ref, sems.at[1]),
    ]
    for c in copies:
        c.start()
    count, tokens, width = query_ref.shape
    per = width // words
    order = ones_where(iota((width, width), 0) == spread(iota((width, width), 1), words, per))
    picks = cand_ref.shape[1]
    repeat = ones_where(iota((picks, width), 0) == iota((picks, width), 1) % picks)
    for c in copies:
        c.wait()
    flat = query_ref[...].reshape(count * tokens, width)
    rows = count * tokens
    out_ref[0:rows, :] = dot(flat, order).astype(jnp.bfloat16)
    ids = cand_ref[...]
    owner = ids // passages
    local = ids - owner * passages
    for i, part in enumerate((owner, local)):
        part = part.astype(jnp.float32).astype(jnp.bfloat16)
        out_ref[rows + i * count : rows + (i + 1) * count, :] = dot(part, repeat).astype(jnp.bfloat16)


def slot_kernel(queries, picks, capacity, rows_ref, slot_ref, rank_ref):
    blocks = rows_ref.shape[0]
    width = rows_ref.shape[2]
    body_rows = rows_ref.shape[1] - 2 * queries
    groups = width // picks
    rows = blocks * queries
    me = lax.axis_index("shard") * lax.axis_size("sub") + lax.axis_index("sub")
    owner = rows_ref[:, body_rows : body_rows + queries, :].reshape(rows, width).astype(jnp.float32)
    local = (
        rows_ref[:, body_rows + queries : body_rows + 2 * queries, :]
        .reshape(rows, width)
        .astype(jnp.float32)
    )
    here = owner == jnp.full((rows, width), me, jnp.int32).astype(jnp.float32)
    here_bf = ones_where(here)
    li = iota((width, width), 0)
    lj = iota((width, width), 1)
    before_lane = ones_where((li < picks) & (li < lj % picks))
    whole_row = ones_where(li < picks)
    ri = iota((rows, rows), 0)
    rj = iota((rows, rows), 1)
    before_row = ones_where((ri // queries == rj // queries) & (rj < ri))
    totals = dot(here_bf, whole_row).astype(jnp.bfloat16)
    rank = dot(here_bf, before_lane) + dot(before_row, totals)
    rank = rank.astype(jnp.int32)
    rank_ref[...] = jnp.where(here, rank, -1)
    lane_group = iota((rows, width), 1) // picks
    which = (iota((rows, width), 0) % queries).astype(jnp.float32)
    padded = slot_ref.shape[0] // 2
    collect = ones_where(iota((padded, rows), 0) == iota((padded, rows), 1) // queries)
    slot_q = jnp.zeros((padded, width), jnp.float32)
    slot_p = jnp.zeros((padded, width), jnp.float32)
    for i in range(-(-capacity // groups)):
        chosen = here & (rank == i * groups + lane_group)
        to_slot = ones_where(lj == i * groups + li // picks)
        got_q = dot(collect, jnp.where(chosen, which, 0.0).astype(jnp.bfloat16))
        got_p = dot(collect, jnp.where(chosen, local, 0.0).astype(jnp.bfloat16))
        slot_q += dot(got_q.astype(jnp.bfloat16), to_slot)
        slot_p += dot(got_p.astype(jnp.bfloat16), to_slot)
    slot_ref[0:padded, :] = slot_q.astype(jnp.int32)
    slot_ref[padded : 2 * padded, :] = slot_p.astype(jnp.int32)


WIDE = 4


def decode_kernel(first, find, start, stop, *refs):
    refs = list(refs)
    ids_hbm, words_hbm, scale_hbm, bucket_hbm = refs[:4]
    del refs[:4]
    if first:
        table_hbm = refs.pop(0)
    else:
        wide = refs.pop(0)
        refs.pop(0)
    if find is not None:
        near_ref = refs.pop(0)
    out_ref = refs.pop(0)
    if first:
        wide = refs.pop(0)
    if find is not None:
        slot_ref, rank_ref = refs[:2]
        del refs[:2]
    rest = refs
    rows, ids_ref, words_ref, scale_bf, scale_ref, bucket_ref, sems = rest[:7]
    mine = pl.ds(start, stop - start)
    copies = [
        pltpu.make_async_copy(ids_hbm.at[mine], ids_ref, sems.at[0]),
        pltpu.make_async_copy(words_hbm.at[mine], words_ref, sems.at[1]),
        pltpu.make_async_copy(scale_hbm, scale_bf, sems.at[2]),
        pltpu.make_async_copy(bucket_hbm, bucket_ref, sems.at[3]),
    ]
    if first:
        table_ref = rest[7]
        parts = 4
        size = table_ref.shape[0] // parts
        loads = [
            pltpu.make_async_copy(
                table_hbm.at[pl.ds(i * size, size)], table_ref.at[pl.ds(i * size, size)], sems.at[4 + i]
            )
            for i in range(parts)
        ]
        for c in loads + copies:
            c.start()
        chunk = 256
        for i in range(parts):
            loads[i].wait()

            def widen(j, _):
                r = pl.ds(pl.multiple_of(i * size + j * chunk, chunk), chunk)
                wide[r, :] = table_ref[r, :].astype(jnp.float32)
                return 0

            lax.fori_loop(0, size // chunk, widen, 0)
    else:
        for c in copies:
            c.start()
    for c in copies:
        c.wait()
    scale_ref[...] = scale_bf[...].astype(jnp.float32)
    slots = ids_ref.shape[1]
    width = wide.shape[1]
    words = words_ref.shape[1]
    per = width // words
    order = ones_where(iota((width, width), 1) == spread(iota((width, width), 0), words, per))
    levels = [
        jnp.broadcast_to(bucket_ref[0:1, i : i + 1].astype(jnp.float32), (words, slots * WIDE))
        for i in range(4)
    ]

    def fetch(p, buf):
        for u in range(WIDE):
            for g in range(slots // 16):
                got = jnp.concatenate(
                    [wide[pl.ds(ids_ref[p + u, g * 16 + i], 1), :] for i in range(16)], axis=0
                )
                r = u * slots + g * 16
                rows[buf, r : r + 16, :] = got.astype(jnp.bfloat16)
                yield

    def build(p, buf, fetching):
        packed = jnp.concatenate([words_ref[p + u] for u in range(WIDE)], axis=1)
        centre = dot(order, rows[buf], ((1,), (1,)))
        parts = []
        for k in range(per):
            for _ in range(WIDE):
                next(fetching, None)
            low = (packed & (1 << (2 * k))) != 0
            high = (packed & (2 << (2 * k))) != 0
            parts.append(
                jnp.where(
                    high,
                    jnp.where(low, levels[3], levels[2]),
                    jnp.where(low, levels[1], levels[0]),
                )
            )
        value = jnp.concatenate(parts, axis=0)
        scale = jnp.concatenate([scale_ref[pl.ds(start + p + u, 1), :] for u in range(WIDE)], axis=1)
        raw = centre + scale * value
        inverse = lax.rsqrt(jnp.sum(raw * raw, axis=0, keepdims=True) + 1e-06)
        out = (raw * inverse).astype(jnp.bfloat16)
        for u in range(WIDE):
            out_ref[start + p + u] = out[:, u * slots : (u + 1) * slots]
        for _ in fetching:
            pass

    for _ in fetch(0, 0):
        pass
    if find is not None:
        slot_kernel(*find, near_ref, slot_ref, rank_ref)

    def step(i, _):
        p = 2 * WIDE * i
        build(p, 0, fetch(p + WIDE, 1))
        build(p + WIDE, 1, fetch(p + 2 * WIDE, 0))
        return 0

    last = stop - start - 2 * WIDE
    for i in range(last // (2 * WIDE)):
        step(i, 0)
    build(last, 0, fetch(last + WIDE, 1))
    build(last + WIDE, 1, iter(()))


def pair_kernel(queries, picks, capacity, ahead, len_hbm, slot_ref, rank_ref, mine_ref, other_ref, emb_ref, *refs):
    refs = list(refs)
    if ahead:
        later_ref = refs.pop(0)
    out_ref = refs.pop(0)
    later_out = refs[: 2 * ahead]
    slot_s, len_s, score, sems = refs[2 * ahead :]
    copies = [
        pltpu.make_async_copy(slot_ref, slot_s, sems.at[0]),
        pltpu.make_async_copy(len_hbm, len_s, sems.at[1]),
    ]
    for c in copies:
        c.start()
    if ahead:
        slot_kernel(queries, picks, capacity, later_ref, *later_out)
    for c in copies:
        c.wait()
    blocks = mine_ref.shape[0]
    width = mine_ref.shape[2]
    tokens = (mine_ref.shape[1] - 2 * queries) // queries
    padded = slot_s.shape[0] // 2
    full_tokens = 2 * tokens
    slots = emb_ref.shape[2]
    lane = iota((full_tokens, slots), 1)
    spot = iota((full_tokens, width), 1)

    def block(b):
        best_all = jnp.zeros((full_tokens, width), jnp.float32)
        for s in range(0, capacity, 2):
            asked = []
            kept = []
            stored = []
            for j in range(s, s + 2):
                p = slot_s[padded + b, j]
                r = pl.ds(pl.multiple_of(slot_s[b, j] * tokens, tokens), tokens)
                asked += [mine_ref[b, r, :], other_ref[b, r, :]]
                stored.append(emb_ref[p])
                kept.append(len_s[p])
            both = dot(jnp.concatenate(asked, axis=0), jnp.concatenate(stored, axis=1))
            for j in range(2):
                similar = both[j * full_tokens : (j + 1) * full_tokens, j * slots : (j + 1) * slots]
                similar = jnp.where(lane < kept[j], similar, masked_floor)
                best = jnp.max(similar, axis=1, keepdims=True)
                best_all = jnp.where(spot == s + j, best, best_all)
        score[pl.ds(b, 1), :] = jnp.sum(best_all, axis=0, keepdims=True) * (1.0 / full_tokens)

    together = math.gcd(blocks, max(1, UNROLLED // capacity))

    def several(i, _):
        for u in range(together):
            block(i * together + u)
        return 0

    lax.fori_loop(0, blocks // together, several, 0)
    groups = width // picks
    lane_group = iota((queries, width), 1) // picks
    for c in range(0, blocks, groups):
        out = jnp.zeros((queries, width), jnp.float32)
        for b in range(c, min(c + groups, blocks)):
            rank = rank_ref[b * queries : (b + 1) * queries, :]
            line = jnp.broadcast_to(score[b : b + 1, :], (queries, width))
            line = jnp.take_along_axis(line, jnp.maximum(rank, 0), axis=1)
            out = jnp.where((rank >= 0) & (lane_group == b - c), line, out)
        out_ref[:, c * picks : c * picks + width] = out


def whole(n, *spaces):
    return [pl.BlockSpec(memory_space=s) for s in spaces] * n


def body(queries, candidates, residuals, centroid_ids, block_scales, lengths, centroids, bucket_weights):
    shards = lax.axis_size("shard")
    halves = lax.axis_size("sub")
    query_count, picks = candidates.shape
    tokens, width = queries.shape[1:]
    passages, slots, words = residuals.shape
    capacity = max(2, 2 * query_count * picks // (shards * halves))

    def swap_shard(x, d):
        return lax.ppermute(x, "shard", [(i, i ^ d) for i in range(shards)])

    def swap_sub(x):
        return lax.ppermute(x, "sub", [(i, i ^ 1) for i in range(halves)])

    payload = pl.pallas_call(
        functools.partial(pack_kernel, words, passages),
        out_shape=jax.ShapeDtypeStruct((query_count * (tokens + 2), width), jnp.bfloat16),
        in_specs=whole(2, pltpu.HBM),
        out_specs=pl.BlockSpec(memory_space=VMEM),
        scratch_shapes=[
            VMEM(queries.shape, queries.dtype),
            VMEM(candidates.shape, candidates.dtype),
            pltpu.SemaphoreType.DMA((2,)),
        ],
        compiler_params=LIMIT,
        cost_estimate=pl.CostEstimate(flops=6 * 10**9, bytes_accessed=0, transcendentals=0),
        name="pack",
    )(queries, candidates)

    stored = (
        centroid_ids,
        jnp.swapaxes(residuals, 1, 2),
        block_scales,
        bucket_weights.reshape(1, 4),
    )
    emb_shape = jax.ShapeDtypeStruct((passages, width, slots), jnp.bfloat16)
    wide_shape = jax.ShapeDtypeStruct(centroids.shape, jnp.float32)

    def slot_shapes(blocks):
        padded = -(-blocks // 8) * 8
        return (
            jax.ShapeDtypeStruct((2 * padded, width), jnp.int32),
            jax.ShapeDtypeStruct((blocks * query_count, width), jnp.int32),
        )

    def decode(start, stop, wide, embedded, near=None):
        first = embedded is None
        extra = (centroids,) if first else (wide, embedded)
        outs = (emb_shape, wide_shape) if first else (emb_shape,)
        specs = whole(5, pltpu.HBM) if first else whole(4, pltpu.HBM) + whole(2, VMEM)
        find = None
        if near is not None:
            find = (query_count, picks, capacity)
            extra += (near,)
            outs += slot_shapes(near.shape[0])
            specs += whole(1, VMEM)
        out = pl.pallas_call(
            functools.partial(decode_kernel, first, find, start, stop),
            out_shape=outs,
            in_specs=specs,
            out_specs=(pl.BlockSpec(memory_space=VMEM),) * len(outs),
            scratch_shapes=[
                VMEM((2, WIDE * slots, width), jnp.bfloat16),
                SMEM((stop - start, slots), jnp.int32),
                VMEM((stop - start, words, slots), jnp.int32),
                VMEM(block_scales.shape, block_scales.dtype),
                VMEM(block_scales.shape, jnp.float32),
                VMEM((1, 4), bucket_weights.dtype),
                pltpu.SemaphoreType.DMA((8 if first else 4,)),
            ]
            + ([VMEM(centroids.shape, centroids.dtype)] if first else []),
            input_output_aliases={} if first else {5: 0},
            compiler_params=LIMIT,
            cost_estimate=pl.CostEstimate(
                flops=(stop - start) * 2 * 10**8, bytes_accessed=0, transcendentals=0
            ),
            name="decode",
        )(*stored, *extra)
        return (out[0], out[1] if first else wide) + tuple(out[2 if first else 1 :])

    def score(found, mine, other, later=None):
        blocks = mine.shape[0]
        padded = -(-blocks // 8) * 8
        lanes = -(-blocks * picks // width) * width
        outs = (jax.ShapeDtypeStruct((query_count, lanes), jnp.float32),)
        operands = (lengths, *found, mine, other, embedded)
        if later is not None:
            outs += slot_shapes(later.shape[0])
            operands += (later,)
        out = pl.pallas_call(
            functools.partial(pair_kernel, query_count, picks, capacity, later is not None),
            out_shape=outs,
            in_specs=whole(1, pltpu.HBM) + whole(len(operands) - 1, VMEM),
            out_specs=(pl.BlockSpec(memory_space=VMEM),) * len(outs),
            scratch_shapes=[
                SMEM((2 * padded, width), jnp.int32),
                SMEM(lengths.shape, jnp.int32),
                VMEM((padded, width), jnp.float32),
                pltpu.SemaphoreType.DMA((2,)),
            ],
            compiler_params=LIMIT,
            cost_estimate=pl.CostEstimate(flops=3 * 10**9, bytes_accessed=0, transcendentals=0),
            name="pairs",
        )(*operands)
        return out[0][:, : blocks * picks], out[1:]

    steps = []
    d = shards // 2
    while d >= 1:
        steps.append(d)
        d //= 2
    unit = 2 * WIDE
    units = passages // unit
    parts = len(steps)
    cuts = [(2 * units * i + parts) // (2 * parts) * unit for i in range(parts + 1)]
    held = payload[None]
    wide = embedded = None
    for i, d in enumerate(steps[:-2]):
        moved = swap_shard(held, d)
        if cuts[i] < cuts[i + 1]:
            embedded, wide = decode(cuts[i], cuts[i + 1], wide, embedded)
            moved, embedded = lax.optimization_barrier((moved, embedded))
        held = jnp.concatenate([held, moved], axis=0)
    moved = swap_shard(held, steps[-2])
    far_a = swap_shard(held, 1)
    if cuts[-3] < cuts[-2]:
        embedded, wide = decode(cuts[-3], cuts[-2], wide, embedded)
        moved, embedded = lax.optimization_barrier((moved, embedded))
    far_b = swap_shard(moved, 1)
    near = jnp.concatenate([held, moved], axis=0)
    embedded, wide, *near_found = decode(cuts[-2], cuts[-1], wide, embedded, near)
    far_b, embedded = lax.optimization_barrier((far_b, embedded))
    far = jnp.concatenate([far_a, far_b], axis=0)
    near_scores, far_found = score(near_found, near, swap_sub(near), far)
    far_scores, _ = score(far_found, far, swap_sub(far))
    total = near_scores + swap_shard(far_scores, 1)
    for d in reversed(steps[:-1]):
        half = total.shape[1] // 2
        total = total[:, :half] + swap_shard(total[:, half:], d)
    return total + swap_sub(total)


def solution(mesh):
    return jax.shard_map(
        body,
        mesh=mesh,
        in_specs=(
            P(("groups", "shard"), "sub", None),
            P(("groups", "shard"), None),
            P(("shard", "sub"), None, None),
            P(("shard", "sub"), None),
            P(("shard", "sub"), None),
            P(("shard", "sub")),
            P(),
            P(),
        ),
        out_specs=P(("groups", "shard"), None),
        check_vma=False,
    )
```

```python
import functools
import math

import jax
import jax.numpy as jnp
from jax import lax
from jax.experimental import pallas as pl
from jax.experimental.pallas import tpu as pltpu
from jax.sharding import PartitionSpec as P

masked_floor = -1000000000.0
UNROLLED = 128
VMEM = pltpu.VMEM
SMEM = pltpu.SMEM
LIMIT = pltpu.CompilerParams(vmem_limit_bytes=40 * 2**20)


def iota(shape, dim):
    return lax.broadcasted_iota(jnp.int32, shape, dim)


def ones_where(mask):
    return jnp.where(mask, 1.0, 0.0).astype(jnp.bfloat16)


def dot(a, b, contract=((1,), (0,))):
    return lax.dot_general(a, b, (contract, ((), ())), preferred_element_type=jnp.float32)


def spread(feature, words, per):
    return per * (feature % words) + feature // words


def pack_kernel(words, passages, query_hbm, cand_hbm, out_ref, query_ref, cand_ref, sems):
    copies = [
        pltpu.make_async_copy(query_hbm, query_ref, sems.at[0]),
        pltpu.make_async_copy(cand_hbm, cand_ref, sems.at[1]),
    ]
    for c in copies:
        c.start()
    count, tokens, width = query_ref.shape
    per = width // words
    order = ones_where(iota((width, width), 0) == spread(iota((width, width), 1), words, per))
    picks = cand_ref.shape[1]
    repeat = ones_where(iota((picks, width), 0) == iota((picks, width), 1) % picks)
    for c in copies:
        c.wait()
    flat = query_ref[...].reshape(count * tokens, width)
    rows = count * tokens
    out_ref[0:rows, :] = dot(flat, order).astype(jnp.bfloat16)
    ids = cand_ref[...]
    owner = ids // passages
    local = ids - owner * passages
    for i, part in enumerate((owner, local)):
        part = part.astype(jnp.float32).astype(jnp.bfloat16)
        out_ref[rows + i * count : rows + (i + 1) * count, :] = dot(part, repeat).astype(jnp.bfloat16)


def slot_kernel(queries, picks, capacity, rows_ref, slot_ref, rank_ref):
    blocks = rows_ref.shape[0]
    width = rows_ref.shape[2]
    body_rows = rows_ref.shape[1] - 2 * queries
    groups = width // picks
    rows = blocks * queries
    me = lax.axis_index("shard") * lax.axis_size("sub") + lax.axis_index("sub")
    owner = rows_ref[:, body_rows : body_rows + queries, :].reshape(rows, width).astype(jnp.float32)
    local = (
        rows_ref[:, body_rows + queries : body_rows + 2 * queries, :]
        .reshape(rows, width)
        .astype(jnp.float32)
    )
    here = owner == jnp.full((rows, width), me, jnp.int32).astype(jnp.float32)
    here_bf = ones_where(here)
    li = iota((width, width), 0)
    lj = iota((width, width), 1)
    before_lane = ones_where((li < picks) & (li < lj % picks))
    whole_row = ones_where(li < picks)
    ri = iota((rows, rows), 0)
    rj = iota((rows, rows), 1)
    before_row = ones_where((ri // queries == rj // queries) & (rj < ri))
    totals = dot(here_bf, whole_row).astype(jnp.bfloat16)
    rank = dot(here_bf, before_lane) + dot(before_row, totals)
    rank = rank.astype(jnp.int32)
    rank_ref[...] = jnp.where(here, rank, -1)
    lane_group = iota((rows, width), 1) // picks
    which = (iota((rows, width), 0) % queries).astype(jnp.float32)
    padded = slot_ref.shape[0] // 2
    collect = ones_where(iota((padded, rows), 0) == iota((padded, rows), 1) // queries)
    slot_q = jnp.zeros((padded, width), jnp.float32)
    slot_p = jnp.zeros((padded, width), jnp.float32)
    for i in range(-(-capacity // groups)):
        chosen = here & (rank == i * groups + lane_group)
        to_slot = ones_where(lj == i * groups + li // picks)
        got_q = dot(collect, jnp.where(chosen, which, 0.0).astype(jnp.bfloat16))
        got_p = dot(collect, jnp.where(chosen, local, 0.0).astype(jnp.bfloat16))
        slot_q += dot(got_q.astype(jnp.bfloat16), to_slot)
        slot_p += dot(got_p.astype(jnp.bfloat16), to_slot)
    slot_ref[0:padded, :] = slot_q.astype(jnp.int32)
    slot_ref[padded : 2 * padded, :] = slot_p.astype(jnp.int32)


WIDE = 4


def decode_kernel(first, find, start, stop, *refs):
    refs = list(refs)
    ids_all, words_ref, scale_bf, bucket_ref = refs[:4]
    del refs[:4]
    if first:
        table_ref = refs.pop(0)
    else:
        wide = refs.pop(0)
        refs.pop(0)
    if find is not None:
        near_ref = refs.pop(0)
    out_ref = refs.pop(0)
    if first:
        wide = refs.pop(0)
    if find is not None:
        slot_ref, rank_ref = refs[:2]
        del refs[:2]
    rows, ids_ref, scale_ref, sem = refs
    copy = pltpu.make_async_copy(ids_all.at[pl.ds(start, stop - start)], ids_ref, sem)
    copy.start()
    scale_ref[...] = scale_bf[...].astype(jnp.float32)
    if first:
        chunk = 512

        def widen(j, _):
            r = pl.ds(pl.multiple_of(j * chunk, chunk), chunk)
            wide[r, :] = table_ref[r, :].astype(jnp.float32)
            return 0

        lax.fori_loop(0, table_ref.shape[0] // chunk, widen, 0)
    if find is not None:
        slot_kernel(*find, near_ref, slot_ref, rank_ref)
    copy.wait()
    slots = ids_ref.shape[1]
    width = wide.shape[1]
    words = words_ref.shape[1]
    per = width // words
    order = ones_where(iota((width, width), 1) == spread(iota((width, width), 0), words, per))
    levels = [
        jnp.broadcast_to(bucket_ref[0:1, i : i + 1].astype(jnp.float32), (words, slots * WIDE))
        for i in range(4)
    ]

    def fetch(p, buf):
        for u in range(WIDE):
            for g in range(slots // 16):
                got = jnp.concatenate(
                    [wide[pl.ds(ids_ref[p + u, g * 16 + i], 1), :] for i in range(16)], axis=0
                )
                r = u * slots + g * 16
                rows[buf, r : r + 16, :] = got.astype(jnp.bfloat16)
                yield

    def build(p, buf, fetching):
        packed = jnp.concatenate([words_ref[start + p + u] for u in range(WIDE)], axis=1)
        centre = dot(order, rows[buf], ((1,), (1,)))
        parts = []
        for k in range(per):
            for _ in range(WIDE):
                next(fetching, None)
            low = (packed & (1 << (2 * k))) != 0
            high = (packed & (2 << (2 * k))) != 0
            parts.append(
                jnp.where(
                    high,
                    jnp.where(low, levels[3], levels[2]),
                    jnp.where(low, levels[1], levels[0]),
                )
            )
        value = jnp.concatenate(parts, axis=0)
        scale = jnp.concatenate([scale_ref[pl.ds(start + p + u, 1), :] for u in range(WIDE)], axis=1)
        raw = centre + scale * value
        inverse = lax.rsqrt(jnp.sum(raw * raw, axis=0, keepdims=True) + 1e-06)
        out = (raw * inverse).astype(jnp.bfloat16)
        for u in range(WIDE):
            out_ref[start + p + u] = out[:, u * slots : (u + 1) * slots]
        for _ in fetching:
            pass

    for _ in fetch(0, 0):
        pass

    def step(i, _):
        p = 2 * WIDE * i
        build(p, 0, fetch(p + WIDE, 1))
        build(p + WIDE, 1, fetch(p + 2 * WIDE, 0))
        return 0

    last = stop - start - 2 * WIDE
    for i in range(last // (2 * WIDE)):
        step(i, 0)
    build(last, 0, fetch(last + WIDE, 1))
    build(last + WIDE, 1, iter(()))


def pair_kernel(queries, picks, capacity, ahead, len_hbm, slot_ref, rank_ref, mine_ref, other_ref, emb_ref, *refs):
    refs = list(refs)
    if ahead:
        later_ref = refs.pop(0)
    out_ref = refs.pop(0)
    later_out = refs[: 2 * ahead]
    slot_s, len_s, score, sems = refs[2 * ahead :]
    copies = [
        pltpu.make_async_copy(slot_ref, slot_s, sems.at[0]),
        pltpu.make_async_copy(len_hbm, len_s, sems.at[1]),
    ]
    for c in copies:
        c.start()
    if ahead:
        slot_kernel(queries, picks, capacity, later_ref, *later_out)
    for c in copies:
        c.wait()
    blocks = mine_ref.shape[0]
    width = mine_ref.shape[2]
    tokens = (mine_ref.shape[1] - 2 * queries) // queries
    padded = slot_s.shape[0] // 2
    full_tokens = 2 * tokens
    slots = emb_ref.shape[2]
    lane = iota((full_tokens, slots), 1)
    spot = iota((full_tokens, width), 1)

    def block(b):
        best_all = jnp.zeros((full_tokens, width), jnp.float32)
        for s in range(0, capacity, 2):
            asked = []
            kept = []
            stored = []
            for j in range(s, s + 2):
                p = slot_s[padded + b, j]
                r = pl.ds(pl.multiple_of(slot_s[b, j] * tokens, tokens), tokens)
                asked += [mine_ref[b, r, :], other_ref[b, r, :]]
                stored.append(emb_ref[p])
                kept.append(len_s[p])
            both = dot(jnp.concatenate(asked, axis=0), jnp.concatenate(stored, axis=1))
            for j in range(2):
                similar = both[j * full_tokens : (j + 1) * full_tokens, j * slots : (j + 1) * slots]
                similar = jnp.where(lane < kept[j], similar, masked_floor)
                best = jnp.max(similar, axis=1, keepdims=True)
                best_all = jnp.where(spot == s + j, best, best_all)
        score[pl.ds(b, 1), :] = jnp.sum(best_all, axis=0, keepdims=True) * (1.0 / full_tokens)

    together = math.gcd(blocks, max(1, UNROLLED // capacity))

    def several(i, _):
        for u in range(together):
            block(i * together + u)
        return 0

    lax.fori_loop(0, blocks // together, several, 0)
    groups = width // picks
    lane_group = iota((queries, width), 1) // picks
    for c in range(0, blocks, groups):
        out = jnp.zeros((queries, width), jnp.float32)
        for b in range(c, min(c + groups, blocks)):
            rank = rank_ref[b * queries : (b + 1) * queries, :]
            line = jnp.broadcast_to(score[b : b + 1, :], (queries, width))
            line = jnp.take_along_axis(line, jnp.maximum(rank, 0), axis=1)
            out = jnp.where((rank >= 0) & (lane_group == b - c), line, out)
        out_ref[:, c * picks : c * picks + width] = out


def whole(n, *spaces):
    return [pl.BlockSpec(memory_space=s) for s in spaces] * n


def body(queries, candidates, residuals, centroid_ids, block_scales, lengths, centroids, bucket_weights):
    shards = lax.axis_size("shard")
    halves = lax.axis_size("sub")
    query_count, picks = candidates.shape
    tokens, width = queries.shape[1:]
    passages, slots, words = residuals.shape
    capacity = max(2, 2 * query_count * picks // (shards * halves))

    def swap_shard(x, d):
        return lax.ppermute(x, "shard", [(i, i ^ d) for i in range(shards)])

    def swap_sub(x):
        return lax.ppermute(x, "sub", [(i, i ^ 1) for i in range(halves)])

    payload = pl.pallas_call(
        functools.partial(pack_kernel, words, passages),
        out_shape=jax.ShapeDtypeStruct((query_count * (tokens + 2), width), jnp.bfloat16),
        in_specs=whole(2, pltpu.HBM),
        out_specs=pl.BlockSpec(memory_space=VMEM),
        scratch_shapes=[
            VMEM(queries.shape, queries.dtype),
            VMEM(candidates.shape, candidates.dtype),
            pltpu.SemaphoreType.DMA((2,)),
        ],
        compiler_params=LIMIT,
        cost_estimate=pl.CostEstimate(flops=6 * 10**9, bytes_accessed=0, transcendentals=0),
        name="pack",
    )(queries, candidates)

    stored = (
        centroid_ids,
        jnp.swapaxes(residuals, 1, 2),
        block_scales,
        bucket_weights.reshape(1, 4),
    )
    emb_shape = jax.ShapeDtypeStruct((passages, width, slots), jnp.bfloat16)
    wide_shape = jax.ShapeDtypeStruct(centroids.shape, jnp.float32)

    def slot_shapes(blocks):
        padded = -(-blocks // 8) * 8
        return (
            jax.ShapeDtypeStruct((2 * padded, width), jnp.int32),
            jax.ShapeDtypeStruct((blocks * query_count, width), jnp.int32),
        )

    def decode(start, stop, wide, embedded, near=None):
        first = embedded is None
        extra = (centroids,) if first else (wide, embedded)
        outs = (emb_shape, wide_shape) if first else (emb_shape,)
        specs = whole(4 + len(extra), VMEM)
        find = None
        if near is not None:
            find = (query_count, picks, capacity)
            extra += (near,)
            outs += slot_shapes(near.shape[0])
            specs += whole(1, VMEM)
        out = pl.pallas_call(
            functools.partial(decode_kernel, first, find, start, stop),
            out_shape=outs,
            in_specs=specs,
            out_specs=(pl.BlockSpec(memory_space=VMEM),) * len(outs),
            scratch_shapes=[
                VMEM((2, WIDE * slots, width), jnp.bfloat16),
                SMEM((stop - start, slots), jnp.int32),
                VMEM(block_scales.shape, jnp.float32),
                pltpu.SemaphoreType.DMA,
            ],
            input_output_aliases={} if first else {5: 0},
            compiler_params=LIMIT,
            cost_estimate=pl.CostEstimate(
                flops=(stop - start) * 2 * 10**8, bytes_accessed=0, transcendentals=0
            ),
            name="decode",
        )(*stored, *extra)
        return (out[0], out[1] if first else wide) + tuple(out[2 if first else 1 :])

    def score(found, mine, other, later=None):
        blocks = mine.shape[0]
        padded = -(-blocks // 8) * 8
        lanes = -(-blocks * picks // width) * width
        outs = (jax.ShapeDtypeStruct((query_count, lanes), jnp.float32),)
        operands = (lengths, *found, mine, other, embedded)
        if later is not None:
            outs += slot_shapes(later.shape[0])
            operands += (later,)
        out = pl.pallas_call(
            functools.partial(pair_kernel, query_count, picks, capacity, later is not None),
            out_shape=outs,
            in_specs=whole(1, pltpu.HBM) + whole(len(operands) - 1, VMEM),
            out_specs=(pl.BlockSpec(memory_space=VMEM),) * len(outs),
            scratch_shapes=[
                SMEM((2 * padded, width), jnp.int32),
                SMEM(lengths.shape, jnp.int32),
                VMEM((padded, width), jnp.float32),
                pltpu.SemaphoreType.DMA((2,)),
            ],
            compiler_params=LIMIT,
            cost_estimate=pl.CostEstimate(flops=3 * 10**9, bytes_accessed=0, transcendentals=0),
            name="pairs",
        )(*operands)
        return out[0][:, : blocks * picks], out[1:]

    steps = []
    d = shards // 2
    while d >= 1:
        steps.append(d)
        d //= 2
    unit = 2 * WIDE
    units = passages // unit
    parts = len(steps)
    cuts = [(2 * units * i + parts) // (2 * parts) * unit for i in range(parts + 1)]
    held = payload[None]
    wide = embedded = None
    for i, d in enumerate(steps[:-2]):
        moved = swap_shard(held, d)
        if cuts[i] < cuts[i + 1]:
            embedded, wide = decode(cuts[i], cuts[i + 1], wide, embedded)
            moved, embedded = lax.optimization_barrier((moved, embedded))
        held = jnp.concatenate([held, moved], axis=0)
    moved = swap_shard(held, steps[-2])
    far_a = swap_shard(held, 1)
    if cuts[-3] < cuts[-2]:
        embedded, wide = decode(cuts[-3], cuts[-2], wide, embedded)
        moved, embedded = lax.optimization_barrier((moved, embedded))
    far_b = swap_shard(moved, 1)
    near = jnp.concatenate([held, moved], axis=0)
    embedded, wide, *near_found = decode(cuts[-2], cuts[-1], wide, embedded, near)
    far_b, embedded = lax.optimization_barrier((far_b, embedded))
    far = jnp.concatenate([far_a, far_b], axis=0)
    near_scores, far_found = score(near_found, near, swap_sub(near), far)
    far_scores, _ = score(far_found, far, swap_sub(far))
    total = near_scores + swap_shard(far_scores, 1)
    for d in reversed(steps[:-1]):
        half = total.shape[1] // 2
        total = total[:, :half] + swap_shard(total[:, half:], d)
    return total + swap_sub(total)


def solution(mesh):
    return jax.shard_map(
        body,
        mesh=mesh,
        in_specs=(
            P(("groups", "shard"), "sub", None),
            P(("groups", "shard"), None),
            P(("shard", "sub"), None, None),
            P(("shard", "sub"), None),
            P(("shard", "sub"), None),
            P(("shard", "sub")),
            P(),
            P(),
        ),
        out_specs=P(("groups", "shard"), None),
        check_vma=False,
    )
```

```python
import functools
import math

import jax
import jax.numpy as jnp
from jax import lax
from jax.experimental import pallas as pl
from jax.experimental.pallas import tpu as pltpu
from jax.sharding import PartitionSpec as P

masked_floor = -1000000000.0
UNROLLED = 128
VMEM = pltpu.VMEM
SMEM = pltpu.SMEM
LIMIT = pltpu.CompilerParams(vmem_limit_bytes=40 * 2**20)


def iota(shape, dim):
    return lax.broadcasted_iota(jnp.int32, shape, dim)


def ones_where(mask):
    return jnp.where(mask, 1.0, 0.0).astype(jnp.bfloat16)


def dot(a, b, contract=((1,), (0,))):
    return lax.dot_general(a, b, (contract, ((), ())), preferred_element_type=jnp.float32)


def spread(feature, words, per):
    return per * (feature % words) + feature // words


def pack_kernel(words, passages, query_hbm, cand_hbm, out_ref, query_ref, cand_ref, sems):
    copies = [
        pltpu.make_async_copy(query_hbm, query_ref, sems.at[0]),
        pltpu.make_async_copy(cand_hbm, cand_ref, sems.at[1]),
    ]
    for c in copies:
        c.start()
    count, tokens, width = query_ref.shape
    per = width // words
    order = ones_where(iota((width, width), 0) == spread(iota((width, width), 1), words, per))
    picks = cand_ref.shape[1]
    for c in copies:
        c.wait()
    flat = query_ref[...].reshape(count * tokens, width)
    rows = count * tokens
    out_ref[0:rows, :] = dot(flat, order).astype(jnp.bfloat16)
    ids = cand_ref[...]
    owner = ids // passages
    local = ids - owner * passages
    row = iota((picks, width), 0)
    lane = iota((picks, width), 1)
    tile = jnp.zeros((count, width), jnp.float32)
    for i, part in enumerate((owner, local)):
        place = ones_where(lane == row + i * picks)
        tile += dot(part.astype(jnp.float32).astype(jnp.bfloat16), place)
    out_ref[rows : rows + count, :] = tile.astype(jnp.bfloat16)


def slot_kernel(queries, picks, capacity, rows_ref, slot_ref, rank_ref):
    blocks = rows_ref.shape[0]
    width = rows_ref.shape[2]
    body_rows = rows_ref.shape[1] - queries
    groups = width // picks
    rows = blocks * queries
    me = lax.axis_index("shard") * lax.axis_size("sub") + lax.axis_index("sub")
    ids = rows_ref[:, body_rows:, :].reshape(rows, width)
    li = iota((width, width), 0)
    lj = iota((width, width), 1)
    owner = dot(ids, ones_where(li == lj % picks))
    local = dot(ids, ones_where(li == picks + lj % picks))
    here = owner == jnp.full((rows, width), me, jnp.int32).astype(jnp.float32)
    here_bf = ones_where(here)
    before_lane = ones_where((li < picks) & (li < lj % picks))
    whole_row = ones_where(li < picks)
    ri = iota((rows, rows), 0)
    rj = iota((rows, rows), 1)
    before_row = ones_where((ri // queries == rj // queries) & (rj < ri))
    totals = dot(here_bf, whole_row).astype(jnp.bfloat16)
    rank = dot(here_bf, before_lane) + dot(before_row, totals)
    rank = rank.astype(jnp.int32)
    rank_ref[...] = jnp.where(here, rank, -1)
    lane_group = iota((rows, width), 1) // picks
    which = (iota((rows, width), 0) % queries).astype(jnp.float32)
    padded = slot_ref.shape[0] // 2
    collect = ones_where(iota((padded, rows), 0) == iota((padded, rows), 1) // queries)
    slot_q = jnp.zeros((padded, width), jnp.float32)
    slot_p = jnp.zeros((padded, width), jnp.float32)
    for i in range(-(-capacity // groups)):
        chosen = here & (rank == i * groups + lane_group)
        to_slot = ones_where(lj == i * groups + li // picks)
        got_q = dot(collect, jnp.where(chosen, which, 0.0).astype(jnp.bfloat16))
        got_p = dot(collect, jnp.where(chosen, local, 0.0).astype(jnp.bfloat16))
        slot_q += dot(got_q.astype(jnp.bfloat16), to_slot)
        slot_p += dot(got_p.astype(jnp.bfloat16), to_slot)
    slot_ref[0:padded, :] = slot_q.astype(jnp.int32)
    slot_ref[padded : 2 * padded, :] = slot_p.astype(jnp.int32)


WIDE = 4


def decode_kernel(first, start, stop, *refs):
    refs = list(refs)
    ids_all, words_ref, scale_bf, bucket_ref = refs[:4]
    del refs[:4]
    if first:
        table_ref = refs.pop(0)
    else:
        wide = refs.pop(0)
        refs.pop(0)
    out_ref = refs.pop(0)
    if first:
        wide = refs.pop(0)
    rows, ids_ref, scale_ref, sem = refs
    copy = pltpu.make_async_copy(ids_all.at[pl.ds(start, stop - start)], ids_ref, sem)
    copy.start()
    scale_ref[...] = scale_bf[...].astype(jnp.float32)
    if first:
        chunk = 512

        def widen(j, _):
            r = pl.ds(pl.multiple_of(j * chunk, chunk), chunk)
            wide[r, :] = table_ref[r, :].astype(jnp.float32)
            return 0

        lax.fori_loop(0, table_ref.shape[0] // chunk, widen, 0)
    copy.wait()
    slots = ids_ref.shape[1]
    width = wide.shape[1]
    words = words_ref.shape[1]
    per = width // words
    order = ones_where(iota((width, width), 1) == spread(iota((width, width), 0), words, per))
    levels = [
        jnp.broadcast_to(bucket_ref[0:1, i : i + 1].astype(jnp.float32), (words, slots * WIDE))
        for i in range(4)
    ]

    def fetch(p, buf):
        for u in range(WIDE):
            for g in range(slots // 16):
                got = jnp.concatenate(
                    [wide[pl.ds(ids_ref[p + u, g * 16 + i], 1), :] for i in range(16)], axis=0
                )
                r = u * slots + g * 16
                rows[buf, r : r + 16, :] = got.astype(jnp.bfloat16)
                yield

    def build(p, buf, fetching):
        packed = jnp.concatenate([words_ref[start + p + u] for u in range(WIDE)], axis=1)
        centre = dot(order, rows[buf], ((1,), (1,)))
        parts = []
        for k in range(per):
            for _ in range(WIDE):
                next(fetching, None)
            low = (packed & (1 << (2 * k))) != 0
            high = (packed & (2 << (2 * k))) != 0
            parts.append(
                jnp.where(
                    high,
                    jnp.where(low, levels[3], levels[2]),
                    jnp.where(low, levels[1], levels[0]),
                )
            )
        value = jnp.concatenate(parts, axis=0)
        scale = jnp.concatenate([scale_ref[pl.ds(start + p + u, 1), :] for u in range(WIDE)], axis=1)
        raw = centre + scale * value
        inverse = lax.rsqrt(jnp.sum(raw * raw, axis=0, keepdims=True) + 1e-06)
        out = (raw * inverse).astype(jnp.bfloat16)
        for u in range(WIDE):
            out_ref[start + p + u] = out[:, u * slots : (u + 1) * slots]
        for _ in fetching:
            pass

    for _ in fetch(0, 0):
        pass

    def step(i, _):
        p = 2 * WIDE * i
        build(p, 0, fetch(p + WIDE, 1))
        build(p + WIDE, 1, fetch(p + 2 * WIDE, 0))
        return 0

    last = stop - start - 2 * WIDE
    for i in range(last // (2 * WIDE)):
        step(i, 0)
    build(last, 0, fetch(last + WIDE, 1))
    build(last + WIDE, 1, iter(()))


def pair_kernel(queries, picks, capacity, ahead, len_hbm, slot_ref, rank_ref, mine_ref, other_ref, emb_ref, *refs):
    refs = list(refs)
    if ahead:
        later_ref = refs.pop(0)
    out_ref = refs.pop(0)
    later_out = refs[: 2 * ahead]
    slot_s, len_s, score, sems = refs[2 * ahead :]
    copies = [
        pltpu.make_async_copy(slot_ref, slot_s, sems.at[0]),
        pltpu.make_async_copy(len_hbm, len_s, sems.at[1]),
    ]
    for c in copies:
        c.start()
    if ahead:
        slot_kernel(queries, picks, capacity, later_ref, *later_out)
    for c in copies:
        c.wait()
    blocks = mine_ref.shape[0]
    width = mine_ref.shape[2]
    tokens = (mine_ref.shape[1] - queries) // queries
    padded = slot_s.shape[0] // 2
    full_tokens = 2 * tokens
    slots = emb_ref.shape[2]
    lane = iota((full_tokens, slots), 1)
    spot = iota((full_tokens, width), 1)

    def block(b):
        best_all = jnp.zeros((full_tokens, width), jnp.float32)
        for s in range(0, capacity, 2):
            asked = []
            kept = []
            stored = []
            for j in range(s, s + 2):
                p = slot_s[padded + b, j]
                r = pl.ds(pl.multiple_of(slot_s[b, j] * tokens, tokens), tokens)
                asked += [mine_ref[b, r, :], other_ref[b, r, :]]
                stored.append(emb_ref[p])
                kept.append(len_s[p])
            both = dot(jnp.concatenate(asked, axis=0), jnp.concatenate(stored, axis=1))
            for j in range(2):
                similar = both[j * full_tokens : (j + 1) * full_tokens, j * slots : (j + 1) * slots]
                similar = jnp.where(lane < kept[j], similar, masked_floor)
                best = jnp.max(similar, axis=1, keepdims=True)
                best_all = jnp.where(spot == s + j, best, best_all)
        score[pl.ds(b, 1), :] = jnp.sum(best_all, axis=0, keepdims=True) * (1.0 / full_tokens)

    together = math.gcd(blocks, max(1, UNROLLED // capacity))

    def several(i, _):
        for u in range(together):
            block(i * together + u)
        return 0

    lax.fori_loop(0, blocks // together, several, 0)
    groups = width // picks
    lane_group = iota((queries, width), 1) // picks
    for c in range(0, blocks, groups):
        out = jnp.zeros((queries, width), jnp.float32)
        for b in range(c, min(c + groups, blocks)):
            rank = rank_ref[b * queries : (b + 1) * queries, :]
            line = jnp.broadcast_to(score[b : b + 1, :], (queries, width))
            line = jnp.take_along_axis(line, jnp.maximum(rank, 0), axis=1)
            out = jnp.where((rank >= 0) & (lane_group == b - c), line, out)
        out_ref[:, c * picks : c * picks + width] = out


def whole(n, *spaces):
    return [pl.BlockSpec(memory_space=s) for s in spaces] * n


def body(queries, candidates, residuals, centroid_ids, block_scales, lengths, centroids, bucket_weights):
    shards = lax.axis_size("shard")
    halves = lax.axis_size("sub")
    query_count, picks = candidates.shape
    tokens, width = queries.shape[1:]
    passages, slots, words = residuals.shape
    capacity = max(2, 2 * query_count * picks // (shards * halves))

    def swap_shard(x, d):
        return lax.ppermute(x, "shard", [(i, i ^ d) for i in range(shards)])

    def swap_sub(x):
        return lax.ppermute(x, "sub", [(i, i ^ 1) for i in range(halves)])

    payload = pl.pallas_call(
        functools.partial(pack_kernel, words, passages),
        out_shape=jax.ShapeDtypeStruct((query_count * (tokens + 1), width), jnp.bfloat16),
        in_specs=whole(2, pltpu.HBM),
        out_specs=pl.BlockSpec(memory_space=VMEM),
        scratch_shapes=[
            VMEM(queries.shape, queries.dtype),
            VMEM(candidates.shape, candidates.dtype),
            pltpu.SemaphoreType.DMA((2,)),
        ],
        compiler_params=LIMIT,
        cost_estimate=pl.CostEstimate(flops=6 * 10**9, bytes_accessed=0, transcendentals=0),
        name="pack",
    )(queries, candidates)

    stored = (
        centroid_ids,
        jnp.swapaxes(residuals, 1, 2),
        block_scales,
        bucket_weights.reshape(1, 4),
    )
    emb_shape = jax.ShapeDtypeStruct((passages, width, slots), jnp.bfloat16)
    wide_shape = jax.ShapeDtypeStruct(centroids.shape, jnp.float32)

    def slot_shapes(blocks):
        padded = -(-blocks // 8) * 8
        return (
            jax.ShapeDtypeStruct((2 * padded, width), jnp.int32),
            jax.ShapeDtypeStruct((blocks * query_count, width), jnp.int32),
        )

    def decode(start, stop, wide, embedded):
        first = embedded is None
        extra = (centroids,) if first else (wide, embedded)
        outs = (emb_shape, wide_shape) if first else (emb_shape,)
        specs = whole(4 + len(extra), VMEM)
        out = pl.pallas_call(
            functools.partial(decode_kernel, first, start, stop),
            out_shape=outs,
            in_specs=specs,
            out_specs=(pl.BlockSpec(memory_space=VMEM),) * len(outs),
            scratch_shapes=[
                VMEM((2, WIDE * slots, width), jnp.bfloat16),
                SMEM((stop - start, slots), jnp.int32),
                VMEM(block_scales.shape, jnp.float32),
                pltpu.SemaphoreType.DMA,
            ],
            input_output_aliases={} if first else {5: 0},
            compiler_params=LIMIT,
            cost_estimate=pl.CostEstimate(
                flops=(stop - start) * 2 * 10**8, bytes_accessed=0, transcendentals=0
            ),
            name="decode",
        )(*stored, *extra)
        return out[0], out[1] if first else wide

    def find(mine):
        return pl.pallas_call(
            functools.partial(slot_kernel, query_count, picks, capacity),
            out_shape=slot_shapes(mine.shape[0]),
            in_specs=whole(1, VMEM),
            out_specs=(pl.BlockSpec(memory_space=VMEM),) * 2,
            compiler_params=LIMIT,
            cost_estimate=pl.CostEstimate(flops=10**9, bytes_accessed=0, transcendentals=0),
            name="slots",
        )(mine)

    def score(found, mine, other, later=None):
        blocks = mine.shape[0]
        padded = -(-blocks // 8) * 8
        lanes = -(-blocks * picks // width) * width
        outs = (jax.ShapeDtypeStruct((query_count, lanes), jnp.float32),)
        operands = (lengths, *found, mine, other, embedded)
        if later is not None:
            outs += slot_shapes(later.shape[0])
            operands += (later,)
        out = pl.pallas_call(
            functools.partial(pair_kernel, query_count, picks, capacity, later is not None),
            out_shape=outs,
            in_specs=whole(1, pltpu.HBM) + whole(len(operands) - 1, VMEM),
            out_specs=(pl.BlockSpec(memory_space=VMEM),) * len(outs),
            scratch_shapes=[
                SMEM((2 * padded, width), jnp.int32),
                SMEM(lengths.shape, jnp.int32),
                VMEM((padded, width), jnp.float32),
                pltpu.SemaphoreType.DMA((2,)),
            ],
            compiler_params=LIMIT,
            cost_estimate=pl.CostEstimate(flops=3 * 10**9, bytes_accessed=0, transcendentals=0),
            name="pairs",
        )(*operands)
        return out[0][:, : blocks * picks], out[1:]

    steps = []
    d = shards // 2
    while d >= 1:
        steps.append(d)
        d //= 2
    unit = 2 * WIDE
    units = passages // unit
    parts = len(steps)
    cuts = [0] + [units * (i + 2) // (parts + 1) * unit for i in range(parts)]
    held = payload[None]
    wide = embedded = None
    for i, d in enumerate(steps[:-2]):
        moved = swap_shard(held, d)
        if cuts[i] < cuts[i + 1]:
            embedded, wide = decode(cuts[i], cuts[i + 1], wide, embedded)
            moved, embedded = lax.optimization_barrier((moved, embedded))
        held = jnp.concatenate([held, moved], axis=0)
    moved = swap_shard(held, steps[-2])
    far_a = swap_shard(held, 1)
    if cuts[-3] < cuts[-2]:
        embedded, wide = decode(cuts[-3], cuts[-2], wide, embedded)
        moved, embedded = lax.optimization_barrier((moved, embedded))
    far_b = swap_shard(moved, 1)
    near = jnp.concatenate([held, moved], axis=0)
    near_other = swap_sub(near)
    embedded, wide = decode(cuts[-2], cuts[-1], wide, embedded)
    far_b, embedded = lax.optimization_barrier((far_b, embedded))
    far = jnp.concatenate([far_a, far_b], axis=0)
    far_scores, near_found = score(find(far), far, swap_sub(far), near)
    near_scores, _ = score(near_found, near, near_other)
    total = near_scores + swap_shard(far_scores, 1)
    for d in reversed(steps[:-1]):
        half = total.shape[1] // 2
        total = total[:, :half] + swap_shard(total[:, half:], d)
    return total + swap_sub(total)


def solution(mesh):
    return jax.shard_map(
        body,
        mesh=mesh,
        in_specs=(
            P(("groups", "shard"), "sub", None),
            P(("groups", "shard"), None),
            P(("shard", "sub"), None, None),
            P(("shard", "sub"), None),
            P(("shard", "sub"), None),
            P(("shard", "sub")),
            P(),
            P(),
        ),
        out_specs=P(("groups", "shard"), None),
        check_vma=False,
    )
```

```python
import functools
import math

import jax
import jax.numpy as jnp
from jax import lax
from jax.experimental import pallas as pl
from jax.experimental.pallas import tpu as pltpu
from jax.sharding import PartitionSpec as P

masked_floor = -1000000000.0
UNROLLED = 128
VMEM = pltpu.VMEM
SMEM = pltpu.SMEM
LIMIT = pltpu.CompilerParams(vmem_limit_bytes=40 * 2**20)


def iota(shape, dim):
    return lax.broadcasted_iota(jnp.int32, shape, dim)


def ones_where(mask):
    return jnp.where(mask, 1.0, 0.0).astype(jnp.bfloat16)


def dot(a, b, contract=((1,), (0,))):
    return lax.dot_general(a, b, (contract, ((), ())), preferred_element_type=jnp.float32)


def spread(feature, words, per):
    return per * (feature % words) + feature // words


def order_kernel(words, out_ref):
    width = out_ref.shape[0]
    source = spread(iota((width, width), 1), words, width // words)
    out_ref[...] = ones_where(iota((width, width), 0) == source)


def pack_kernel(passages, query_ref, cand_ref, order_ref, out_ref):
    count, tokens, width = query_ref.shape
    picks = cand_ref.shape[1]
    flat = query_ref[...].reshape(count * tokens, width)
    rows = count * tokens
    out_ref[0:rows, :] = dot(flat, order_ref[...]).astype(jnp.bfloat16)
    ids = cand_ref[...]
    owner = ids // passages
    local = ids - owner * passages
    row = iota((picks, width), 0)
    lane = iota((picks, width), 1)
    tile = jnp.zeros((count, width), jnp.float32)
    for i, part in enumerate((owner, local)):
        place = ones_where(lane == row + i * picks)
        tile += dot(part.astype(jnp.float32).astype(jnp.bfloat16), place)
    out_ref[rows : rows + count, :] = tile.astype(jnp.bfloat16)


def slot_kernel(queries, picks, capacity, rows_ref, slot_ref, rank_ref):
    blocks = rows_ref.shape[0]
    width = rows_ref.shape[2]
    body_rows = rows_ref.shape[1] - queries
    groups = width // picks
    rows = blocks * queries
    me = lax.axis_index("shard") * lax.axis_size("sub") + lax.axis_index("sub")
    ids = rows_ref[:, body_rows:, :].reshape(rows, width)
    li = iota((width, width), 0)
    lj = iota((width, width), 1)
    owner = dot(ids, ones_where(li == lj % picks))
    local = dot(ids, ones_where(li == picks + lj % picks))
    here = owner == jnp.full((rows, width), me, jnp.int32).astype(jnp.float32)
    here_bf = ones_where(here)
    before_lane = ones_where((li < picks) & (li < lj % picks))
    whole_row = ones_where(li < picks)
    ri = iota((rows, rows), 0)
    rj = iota((rows, rows), 1)
    before_row = ones_where((ri // queries == rj // queries) & (rj < ri))
    totals = dot(here_bf, whole_row).astype(jnp.bfloat16)
    rank = dot(here_bf, before_lane) + dot(before_row, totals)
    rank = rank.astype(jnp.int32)
    rank_ref[...] = jnp.where(here, rank, -1)
    lane_group = iota((rows, width), 1) // picks
    which = (iota((rows, width), 0) % queries).astype(jnp.float32)
    padded = slot_ref.shape[0] // 2
    collect = ones_where(iota((padded, rows), 0) == iota((padded, rows), 1) // queries)
    slot_q = jnp.zeros((padded, width), jnp.float32)
    slot_p = jnp.zeros((padded, width), jnp.float32)
    for i in range(-(-capacity // groups)):
        chosen = here & (rank == i * groups + lane_group)
        to_slot = ones_where(lj == i * groups + li // picks)
        got_q = dot(collect, jnp.where(chosen, which, 0.0).astype(jnp.bfloat16))
        got_p = dot(collect, jnp.where(chosen, local, 0.0).astype(jnp.bfloat16))
        slot_q += dot(got_q.astype(jnp.bfloat16), to_slot)
        slot_p += dot(got_p.astype(jnp.bfloat16), to_slot)
    slot_ref[0:padded, :] = slot_q.astype(jnp.int32)
    slot_ref[padded : 2 * padded, :] = slot_p.astype(jnp.int32)


WIDE = 4


def decode_kernel(first, start, stop, *refs):
    refs = list(refs)
    ids_all, words_ref, scale_bf, bucket_ref = refs[:4]
    del refs[:4]
    if first:
        table_ref = refs.pop(0)
    else:
        wide = refs.pop(0)
        refs.pop(0)
    out_ref = refs.pop(0)
    if first:
        wide = refs.pop(0)
    rows, ids_ref, scale_ref, sem = refs
    copy = pltpu.make_async_copy(ids_all.at[pl.ds(start, stop - start)], ids_ref, sem)
    copy.start()
    scale_ref[...] = scale_bf[...].astype(jnp.float32)
    if first:
        chunk = 512

        def widen(j, _):
            r = pl.ds(pl.multiple_of(j * chunk, chunk), chunk)
            wide[r, :] = table_ref[r, :].astype(jnp.float32)
            return 0

        lax.fori_loop(0, table_ref.shape[0] // chunk, widen, 0)
    copy.wait()
    slots = ids_ref.shape[1]
    width = wide.shape[1]
    words = words_ref.shape[1]
    per = width // words
    order = ones_where(iota((width, width), 1) == spread(iota((width, width), 0), words, per))
    levels = [
        jnp.broadcast_to(bucket_ref[0:1, i : i + 1].astype(jnp.float32), (words, slots * WIDE))
        for i in range(4)
    ]

    def fetch(p, buf):
        for u in range(WIDE):
            for g in range(slots // 16):
                got = jnp.concatenate(
                    [wide[pl.ds(ids_ref[p + u, g * 16 + i], 1), :] for i in range(16)], axis=0
                )
                r = u * slots + g * 16
                rows[buf, r : r + 16, :] = got.astype(jnp.bfloat16)
                yield

    def build(p, buf, fetching):
        packed = jnp.concatenate([words_ref[start + p + u] for u in range(WIDE)], axis=1)
        centre = dot(order, rows[buf], ((1,), (1,)))
        parts = []
        for k in range(per):
            for _ in range(WIDE):
                next(fetching, None)
            low = (packed & (1 << (2 * k))) != 0
            high = (packed & (2 << (2 * k))) != 0
            parts.append(
                jnp.where(
                    high,
                    jnp.where(low, levels[3], levels[2]),
                    jnp.where(low, levels[1], levels[0]),
                )
            )
        value = jnp.concatenate(parts, axis=0)
        scale = jnp.concatenate([scale_ref[pl.ds(start + p + u, 1), :] for u in range(WIDE)], axis=1)
        raw = centre + scale * value
        inverse = lax.rsqrt(jnp.sum(raw * raw, axis=0, keepdims=True) + 1e-06)
        out = (raw * inverse).astype(jnp.bfloat16)
        for u in range(WIDE):
            out_ref[start + p + u] = out[:, u * slots : (u + 1) * slots]
        for _ in fetching:
            pass

    for _ in fetch(0, 0):
        pass

    def step(i, _):
        p = 2 * WIDE * i
        build(p, 0, fetch(p + WIDE, 1))
        build(p + WIDE, 1, fetch(p + 2 * WIDE, 0))
        return 0

    last = stop - start - 2 * WIDE
    for i in range(last // (2 * WIDE)):
        step(i, 0)
    build(last, 0, fetch(last + WIDE, 1))
    build(last + WIDE, 1, iter(()))


def pair_kernel(queries, picks, capacity, ahead, len_hbm, slot_ref, rank_ref, mine_ref, other_ref, emb_ref, *refs):
    refs = list(refs)
    if ahead:
        later_ref = refs.pop(0)
    out_ref = refs.pop(0)
    later_out = refs[: 2 * ahead]
    slot_s, len_s, score, sems = refs[2 * ahead :]
    copies = [
        pltpu.make_async_copy(slot_ref, slot_s, sems.at[0]),
        pltpu.make_async_copy(len_hbm, len_s, sems.at[1]),
    ]
    for c in copies:
        c.start()
    if ahead:
        slot_kernel(queries, picks, capacity, later_ref, *later_out)
    for c in copies:
        c.wait()
    blocks = mine_ref.shape[0]
    width = mine_ref.shape[2]
    tokens = (mine_ref.shape[1] - queries) // queries
    padded = slot_s.shape[0] // 2
    full_tokens = 2 * tokens
    slots = emb_ref.shape[2]
    lane = iota((full_tokens, slots), 1)
    spot = iota((full_tokens, width), 1)

    def block(b):
        best_all = jnp.zeros((full_tokens, width), jnp.float32)
        for s in range(0, capacity, 2):
            asked = []
            kept = []
            stored = []
            for j in range(s, s + 2):
                p = slot_s[padded + b, j]
                r = pl.ds(pl.multiple_of(slot_s[b, j] * tokens, tokens), tokens)
                asked += [mine_ref[b, r, :], other_ref[b, r, :]]
                stored.append(emb_ref[p])
                kept.append(len_s[p])
            both = dot(jnp.concatenate(asked, axis=0), jnp.concatenate(stored, axis=1))
            for j in range(2):
                similar = both[j * full_tokens : (j + 1) * full_tokens, j * slots : (j + 1) * slots]
                similar = jnp.where(lane < kept[j], similar, masked_floor)
                best = jnp.max(similar, axis=1, keepdims=True)
                best_all = jnp.where(spot == s + j, best, best_all)
        score[pl.ds(b, 1), :] = jnp.sum(best_all, axis=0, keepdims=True) * (1.0 / full_tokens)

    together = math.gcd(blocks, max(1, UNROLLED // capacity))

    def several(i, _):
        for u in range(together):
            block(i * together + u)
        return 0

    lax.fori_loop(0, blocks // together, several, 0)
    groups = width // picks
    lane_group = iota((queries, width), 1) // picks
    for c in range(0, blocks, groups):
        out = jnp.zeros((queries, width), jnp.float32)
        for b in range(c, min(c + groups, blocks)):
            rank = rank_ref[b * queries : (b + 1) * queries, :]
            line = jnp.broadcast_to(score[b : b + 1, :], (queries, width))
            line = jnp.take_along_axis(line, jnp.maximum(rank, 0), axis=1)
            out = jnp.where((rank >= 0) & (lane_group == b - c), line, out)
        out_ref[:, c * picks : c * picks + width] = out


def whole(n, *spaces):
    return [pl.BlockSpec(memory_space=s) for s in spaces] * n


def body(queries, candidates, residuals, centroid_ids, block_scales, lengths, centroids, bucket_weights):
    shards = lax.axis_size("shard")
    halves = lax.axis_size("sub")
    query_count, picks = candidates.shape
    tokens, width = queries.shape[1:]
    passages, slots, words = residuals.shape
    capacity = max(2, 2 * query_count * picks // (shards * halves))

    def swap_shard(x, d):
        return lax.ppermute(x, "shard", [(i, i ^ d) for i in range(shards)])

    def swap_sub(x):
        return lax.ppermute(x, "sub", [(i, i ^ 1) for i in range(halves)])

    order = pl.pallas_call(
        functools.partial(order_kernel, words),
        out_shape=jax.ShapeDtypeStruct((width, width), jnp.bfloat16),
        out_specs=pl.BlockSpec(memory_space=VMEM),
        compiler_params=LIMIT,
        cost_estimate=pl.CostEstimate(flops=6 * 10**9, bytes_accessed=0, transcendentals=0),
        name="order",
    )()
    payload = pl.pallas_call(
        functools.partial(pack_kernel, passages),
        out_shape=jax.ShapeDtypeStruct((query_count * (tokens + 1), width), jnp.bfloat16),
        in_specs=whole(3, VMEM),
        out_specs=pl.BlockSpec(memory_space=VMEM),
        compiler_params=LIMIT,
        cost_estimate=pl.CostEstimate(flops=6 * 10**9, bytes_accessed=0, transcendentals=0),
        name="pack",
    )(queries, candidates, order)

    stored = (
        centroid_ids,
        jnp.swapaxes(residuals, 1, 2),
        block_scales,
        bucket_weights.reshape(1, 4),
    )
    emb_shape = jax.ShapeDtypeStruct((passages, width, slots), jnp.bfloat16)
    wide_shape = jax.ShapeDtypeStruct(centroids.shape, jnp.float32)

    def slot_shapes(blocks):
        padded = -(-blocks // 8) * 8
        return (
            jax.ShapeDtypeStruct((2 * padded, width), jnp.int32),
            jax.ShapeDtypeStruct((blocks * query_count, width), jnp.int32),
        )

    def decode(start, stop, wide, embedded):
        first = embedded is None
        extra = (centroids,) if first else (wide, embedded)
        outs = (emb_shape, wide_shape) if first else (emb_shape,)
        specs = whole(4 + len(extra), VMEM)
        out = pl.pallas_call(
            functools.partial(decode_kernel, first, start, stop),
            out_shape=outs,
            in_specs=specs,
            out_specs=(pl.BlockSpec(memory_space=VMEM),) * len(outs),
            scratch_shapes=[
                VMEM((2, WIDE * slots, width), jnp.bfloat16),
                SMEM((stop - start, slots), jnp.int32),
                VMEM(block_scales.shape, jnp.float32),
                pltpu.SemaphoreType.DMA,
            ],
            input_output_aliases={} if first else {5: 0},
            compiler_params=LIMIT,
            cost_estimate=pl.CostEstimate(
                flops=(stop - start) * 2 * 10**8, bytes_accessed=0, transcendentals=0
            ),
            name="decode",
        )(*stored, *extra)
        return out[0], out[1] if first else wide

    def find(mine):
        return pl.pallas_call(
            functools.partial(slot_kernel, query_count, picks, capacity),
            out_shape=slot_shapes(mine.shape[0]),
            in_specs=whole(1, VMEM),
            out_specs=(pl.BlockSpec(memory_space=VMEM),) * 2,
            compiler_params=LIMIT,
            cost_estimate=pl.CostEstimate(flops=10**9, bytes_accessed=0, transcendentals=0),
            name="slots",
        )(mine)

    def score(found, mine, other, later=None):
        blocks = mine.shape[0]
        padded = -(-blocks // 8) * 8
        lanes = -(-blocks * picks // width) * width
        outs = (jax.ShapeDtypeStruct((query_count, lanes), jnp.float32),)
        operands = (lengths, *found, mine, other, embedded)
        if later is not None:
            outs += slot_shapes(later.shape[0])
            operands += (later,)
        out = pl.pallas_call(
            functools.partial(pair_kernel, query_count, picks, capacity, later is not None),
            out_shape=outs,
            in_specs=whole(1, pltpu.HBM) + whole(len(operands) - 1, VMEM),
            out_specs=(pl.BlockSpec(memory_space=VMEM),) * len(outs),
            scratch_shapes=[
                SMEM((2 * padded, width), jnp.int32),
                SMEM(lengths.shape, jnp.int32),
                VMEM((padded, width), jnp.float32),
                pltpu.SemaphoreType.DMA((2,)),
            ],
            compiler_params=LIMIT,
            cost_estimate=pl.CostEstimate(flops=3 * 10**9, bytes_accessed=0, transcendentals=0),
            name="pairs",
        )(*operands)
        return out[0][:, : blocks * picks], out[1:]

    steps = []
    d = shards // 2
    while d >= 1:
        steps.append(d)
        d //= 2
    unit = 2 * WIDE
    units = passages // unit
    parts = len(steps)
    cuts = [(2 * units * i + parts) // (2 * parts) * unit for i in range(parts + 1)]
    held = payload[None]
    wide = embedded = None
    for i, d in enumerate(steps[:-2]):
        moved = swap_shard(held, d)
        if cuts[i] < cuts[i + 1]:
            embedded, wide = decode(cuts[i], cuts[i + 1], wide, embedded)
            moved, embedded = lax.optimization_barrier((moved, embedded))
        held = jnp.concatenate([held, moved], axis=0)
    moved = swap_shard(held, steps[-2])
    far_a = swap_shard(held, 1)
    if cuts[-3] < cuts[-2]:
        embedded, wide = decode(cuts[-3], cuts[-2], wide, embedded)
        moved, embedded = lax.optimization_barrier((moved, embedded))
    far_b = swap_shard(moved, 1)
    near = jnp.concatenate([held, moved], axis=0)
    near_other = swap_sub(near)
    embedded, wide = decode(cuts[-2], cuts[-1], wide, embedded)
    far_b, embedded = lax.optimization_barrier((far_b, embedded))
    far = jnp.concatenate([far_a, far_b], axis=0)
    far_scores, near_found = score(find(far), far, swap_sub(far), near)
    near_scores, _ = score(near_found, near, near_other)
    total = near_scores + swap_shard(far_scores, 1)
    for d in reversed(steps[:-1]):
        half = total.shape[1] // 2
        total = total[:, :half] + swap_shard(total[:, half:], d)
    return total + swap_sub(total)


def solution(mesh):
    return jax.shard_map(
        body,
        mesh=mesh,
        in_specs=(
            P(("groups", "shard"), "sub", None),
            P(("groups", "shard"), None),
            P(("shard", "sub"), None, None),
            P(("shard", "sub"), None),
            P(("shard", "sub"), None),
            P(("shard", "sub")),
            P(),
            P(),
        ),
        out_specs=P(("groups", "shard"), None),
        check_vma=False,
    )
```

```python
import functools
import math

import jax
import jax.numpy as jnp
from jax import lax
from jax.experimental import pallas as pl
from jax.experimental.pallas import tpu as pltpu
from jax.sharding import PartitionSpec as P

masked_floor = -1000000000.0
UNROLLED = 128
VMEM = pltpu.VMEM
SMEM = pltpu.SMEM
LIMIT = pltpu.CompilerParams(vmem_limit_bytes=40 * 2**20)


def iota(shape, dim):
    return lax.broadcasted_iota(jnp.int32, shape, dim)


def ones_where(mask):
    return jnp.where(mask, 1.0, 0.0).astype(jnp.bfloat16)


def dot(a, b, contract=((1,), (0,))):
    return lax.dot_general(a, b, (contract, ((), ())), preferred_element_type=jnp.float32)


def spread(feature, words, per):
    return per * (feature % words) + feature // words


def order_kernel(words, out_ref):
    width = out_ref.shape[0]
    source = spread(iota((width, width), 1), words, width // words)
    out_ref[...] = ones_where(iota((width, width), 0) == source)


def pack_kernel(passages, query_ref, cand_ref, order_ref, out_ref):
    count, tokens, width = query_ref.shape
    picks = cand_ref.shape[1]
    flat = query_ref[...].reshape(count * tokens, width)
    rows = count * tokens
    out_ref[0:rows, :] = dot(flat, order_ref[...]).astype(jnp.bfloat16)
    ids = cand_ref[...]
    owner = ids // passages
    local = ids - owner * passages
    row = iota((picks, width), 0)
    lane = iota((picks, width), 1)
    tile = jnp.zeros((count, width), jnp.float32)
    for i, part in enumerate((owner, local)):
        place = ones_where(lane == row + i * picks)
        tile += dot(part.astype(jnp.float32).astype(jnp.bfloat16), place)
    out_ref[rows : rows + count, :] = tile.astype(jnp.bfloat16)


def slot_kernel(queries, picks, capacity, rows_ref, slot_ref, rank_ref):
    blocks = rows_ref.shape[0]
    width = rows_ref.shape[2]
    body_rows = rows_ref.shape[1] - queries
    groups = width // picks
    rows = blocks * queries
    me = lax.axis_index("shard") * lax.axis_size("sub") + lax.axis_index("sub")
    ids = rows_ref[:, body_rows:, :].reshape(rows, width)
    li = iota((width, width), 0)
    lj = iota((width, width), 1)
    owner = dot(ids, ones_where(li == lj % picks))
    local = dot(ids, ones_where(li == picks + lj % picks))
    here = owner == jnp.full((rows, width), me, jnp.int32).astype(jnp.float32)
    here_bf = ones_where(here)
    before_lane = ones_where((li < picks) & (li < lj % picks))
    whole_row = ones_where(li < picks)
    ri = iota((rows, rows), 0)
    rj = iota((rows, rows), 1)
    before_row = ones_where((ri // queries == rj // queries) & (rj < ri))
    totals = dot(here_bf, whole_row).astype(jnp.bfloat16)
    rank = dot(here_bf, before_lane) + dot(before_row, totals)
    rank = rank.astype(jnp.int32)
    rank_ref[...] = jnp.where(here, rank, -1)
    lane_group = iota((rows, width), 1) // picks
    which = (iota((rows, width), 0) % queries).astype(jnp.float32)
    padded = slot_ref.shape[0] // 2
    collect = ones_where(iota((padded, rows), 0) == iota((padded, rows), 1) // queries)
    slot_q = jnp.zeros((padded, width), jnp.float32)
    slot_p = jnp.zeros((padded, width), jnp.float32)
    for i in range(-(-capacity // groups)):
        chosen = here & (rank == i * groups + lane_group)
        to_slot = ones_where(lj == i * groups + li // picks)
        got_q = dot(collect, jnp.where(chosen, which, 0.0).astype(jnp.bfloat16))
        got_p = dot(collect, jnp.where(chosen, local, 0.0).astype(jnp.bfloat16))
        slot_q += dot(got_q.astype(jnp.bfloat16), to_slot)
        slot_p += dot(got_p.astype(jnp.bfloat16), to_slot)
    slot_ref[0:padded, :] = slot_q.astype(jnp.int32)
    slot_ref[padded : 2 * padded, :] = slot_p.astype(jnp.int32)


WIDE = 4


def decode_kernel(first, start, stop, *refs):
    refs = list(refs)
    ids_all, words_ref, scale_bf, bucket_ref = refs[:4]
    del refs[:4]
    if first:
        table_ref = refs.pop(0)
    else:
        wide = refs.pop(0)
        refs.pop(0)
    out_ref = refs.pop(0)
    if first:
        wide = refs.pop(0)
    rows, ids_ref, scale_ref, sem = refs
    copy = pltpu.make_async_copy(ids_all.at[pl.ds(start, stop - start)], ids_ref, sem)
    copy.start()
    scale_ref[...] = scale_bf[...].astype(jnp.float32)
    if first:
        chunk = 512

        def widen(j, _):
            r = pl.ds(pl.multiple_of(j * chunk, chunk), chunk)
            wide[r, :] = table_ref[r, :].astype(jnp.float32)
            return 0

        lax.fori_loop(0, table_ref.shape[0] // chunk, widen, 0)
    copy.wait()
    slots = ids_ref.shape[1]
    width = wide.shape[1]
    words = words_ref.shape[1]
    per = width // words
    order = ones_where(iota((width, width), 1) == spread(iota((width, width), 0), words, per))
    levels = [
        jnp.broadcast_to(bucket_ref[0:1, i : i + 1].astype(jnp.float32), (words, slots * WIDE))
        for i in range(4)
    ]

    def fetch(p, buf):
        for u in range(WIDE):
            for g in range(slots // 16):
                got = jnp.concatenate(
                    [wide[pl.ds(ids_ref[p + u, g * 16 + i], 1), :] for i in range(16)], axis=0
                )
                r = u * slots + g * 16
                rows[buf, r : r + 16, :] = got.astype(jnp.bfloat16)
                yield

    def build(p, buf, fetching):
        packed = jnp.concatenate([words_ref[start + p + u] for u in range(WIDE)], axis=1)
        centre = dot(order, rows[buf], ((1,), (1,)))
        parts = []
        for k in range(per):
            for _ in range(WIDE):
                next(fetching, None)
            low = (packed & (1 << (2 * k))) != 0
            high = (packed & (2 << (2 * k))) != 0
            parts.append(
                jnp.where(
                    high,
                    jnp.where(low, levels[3], levels[2]),
                    jnp.where(low, levels[1], levels[0]),
                )
            )
        value = jnp.concatenate(parts, axis=0)
        scale = jnp.concatenate([scale_ref[pl.ds(start + p + u, 1), :] for u in range(WIDE)], axis=1)
        raw = centre + scale * value
        inverse = lax.rsqrt(jnp.sum(raw * raw, axis=0, keepdims=True) + 1e-06)
        out = (raw * inverse).astype(jnp.bfloat16)
        for u in range(WIDE):
            out_ref[start + p + u] = out[:, u * slots : (u + 1) * slots]
        for _ in fetching:
            pass

    for _ in fetch(0, 0):
        pass

    def step(i, _):
        p = 2 * WIDE * i
        build(p, 0, fetch(p + WIDE, 1))
        build(p + WIDE, 1, fetch(p + 2 * WIDE, 0))
        return 0

    last = stop - start - 2 * WIDE
    for i in range(last // (2 * WIDE)):
        step(i, 0)
    build(last, 0, fetch(last + WIDE, 1))
    build(last + WIDE, 1, iter(()))


def pair_kernel(queries, picks, capacity, ahead, len_hbm, slot_ref, rank_ref, mine_ref, other_ref, emb_ref, *refs):
    refs = list(refs)
    if ahead:
        later_ref = refs.pop(0)
    out_ref = refs.pop(0)
    later_out = refs[: 2 * ahead]
    slot_s, len_s, score, sems = refs[2 * ahead :]
    copies = [
        pltpu.make_async_copy(slot_ref, slot_s, sems.at[0]),
        pltpu.make_async_copy(len_hbm, len_s, sems.at[1]),
    ]
    for c in copies:
        c.start()
    if ahead:
        slot_kernel(queries, picks, capacity, later_ref, *later_out)
    for c in copies:
        c.wait()
    blocks = mine_ref.shape[0]
    width = mine_ref.shape[2]
    tokens = (mine_ref.shape[1] - queries) // queries
    padded = slot_s.shape[0] // 2
    full_tokens = 2 * tokens
    slots = emb_ref.shape[2]
    lane = iota((full_tokens, slots), 1)
    spot = iota((full_tokens, width), 1)

    def block(b):
        best_all = jnp.zeros((full_tokens, width), jnp.float32)
        for s in range(0, capacity, 2):
            asked = []
            kept = []
            stored = []
            for j in range(s, s + 2):
                p = slot_s[padded + b, j]
                r = pl.ds(pl.multiple_of(slot_s[b, j] * tokens, tokens), tokens)
                asked += [mine_ref[b, r, :], other_ref[b, r, :]]
                stored.append(emb_ref[p])
                kept.append(len_s[p])
            both = dot(jnp.concatenate(asked, axis=0), jnp.concatenate(stored, axis=1))
            for j in range(2):
                similar = both[j * full_tokens : (j + 1) * full_tokens, j * slots : (j + 1) * slots]
                similar = jnp.where(lane < kept[j], similar, masked_floor)
                best = jnp.max(similar, axis=1, keepdims=True)
                best_all = jnp.where(spot == s + j, best, best_all)
        score[pl.ds(b, 1), :] = jnp.sum(best_all, axis=0, keepdims=True) * (1.0 / full_tokens)

    together = math.gcd(blocks, max(1, UNROLLED // capacity))

    def several(i, _):
        for u in range(together):
            block(i * together + u)
        return 0

    lax.fori_loop(0, blocks // together, several, 0)
    groups = width // picks
    lane_group = iota((queries, width), 1) // picks
    for c in range(0, blocks, groups):
        out = jnp.zeros((queries, width), jnp.float32)
        for b in range(c, min(c + groups, blocks)):
            rank = rank_ref[b * queries : (b + 1) * queries, :]
            line = jnp.broadcast_to(score[b : b + 1, :], (queries, width))
            line = jnp.take_along_axis(line, jnp.maximum(rank, 0), axis=1)
            out = jnp.where((rank >= 0) & (lane_group == b - c), line, out)
        out_ref[:, c * picks : c * picks + width] = out


def whole(n, *spaces):
    return [pl.BlockSpec(memory_space=s) for s in spaces] * n


def body(queries, candidates, residuals, centroid_ids, block_scales, lengths, centroids, bucket_weights):
    shards = lax.axis_size("shard")
    halves = lax.axis_size("sub")
    query_count, picks = candidates.shape
    tokens, width = queries.shape[1:]
    passages, slots, words = residuals.shape
    capacity = max(2, 2 * query_count * picks // (shards * halves))

    def swap_shard(x, d):
        return lax.ppermute(x, "shard", [(i, i ^ d) for i in range(shards)])

    def swap_sub(x):
        return lax.ppermute(x, "sub", [(i, i ^ 1) for i in range(halves)])

    order = pl.pallas_call(
        functools.partial(order_kernel, words),
        out_shape=jax.ShapeDtypeStruct((width, width), jnp.bfloat16),
        out_specs=pl.BlockSpec(memory_space=VMEM),
        compiler_params=LIMIT,
        cost_estimate=pl.CostEstimate(flops=6 * 10**9, bytes_accessed=0, transcendentals=0),
        name="order",
    )()
    payload = pl.pallas_call(
        functools.partial(pack_kernel, passages),
        out_shape=jax.ShapeDtypeStruct((query_count * (tokens + 1), width), jnp.bfloat16),
        in_specs=whole(3, VMEM),
        out_specs=pl.BlockSpec(memory_space=VMEM),
        compiler_params=LIMIT,
        cost_estimate=pl.CostEstimate(flops=6 * 10**9, bytes_accessed=0, transcendentals=0),
        name="pack",
    )(queries, candidates, order)

    stored = (
        centroid_ids,
        jnp.swapaxes(residuals, 1, 2),
        block_scales,
        bucket_weights.reshape(1, 4),
    )
    emb_shape = jax.ShapeDtypeStruct((passages, width, slots), jnp.bfloat16)
    wide_shape = jax.ShapeDtypeStruct(centroids.shape, jnp.float32)

    def slot_shapes(blocks):
        padded = -(-blocks // 8) * 8
        return (
            jax.ShapeDtypeStruct((2 * padded, width), jnp.int32),
            jax.ShapeDtypeStruct((blocks * query_count, width), jnp.int32),
        )

    def decode(start, stop, wide, embedded):
        first = embedded is None
        extra = (centroids,) if first else (wide, embedded)
        outs = (emb_shape, wide_shape) if first else (emb_shape,)
        specs = whole(4 + len(extra), VMEM)
        out = pl.pallas_call(
            functools.partial(decode_kernel, first, start, stop),
            out_shape=outs,
            in_specs=specs,
            out_specs=(pl.BlockSpec(memory_space=VMEM),) * len(outs),
            scratch_shapes=[
                VMEM((2, WIDE * slots, width), jnp.bfloat16),
                SMEM((stop - start, slots), jnp.int32),
                VMEM(block_scales.shape, jnp.float32),
                pltpu.SemaphoreType.DMA,
            ],
            input_output_aliases={} if first else {5: 0},
            compiler_params=LIMIT,
            cost_estimate=pl.CostEstimate(
                flops=(stop - start) * 2 * 10**8, bytes_accessed=0, transcendentals=0
            ),
            name="decode",
        )(*stored, *extra)
        return out[0], out[1] if first else wide

    def find(mine):
        return pl.pallas_call(
            functools.partial(slot_kernel, query_count, picks, capacity),
            out_shape=slot_shapes(mine.shape[0]),
            in_specs=whole(1, VMEM),
            out_specs=(pl.BlockSpec(memory_space=VMEM),) * 2,
            compiler_params=LIMIT,
            cost_estimate=pl.CostEstimate(flops=10**9, bytes_accessed=0, transcendentals=0),
            name="slots",
        )(mine)

    def score(found, mine, other, later=None):
        blocks = mine.shape[0]
        padded = -(-blocks // 8) * 8
        lanes = -(-blocks * picks // width) * width
        outs = (jax.ShapeDtypeStruct((query_count, lanes), jnp.float32),)
        operands = (lengths, *found, mine, other, embedded)
        if later is not None:
            outs += slot_shapes(later.shape[0])
            operands += (later,)
        out = pl.pallas_call(
            functools.partial(pair_kernel, query_count, picks, capacity, later is not None),
            out_shape=outs,
            in_specs=whole(1, pltpu.HBM) + whole(len(operands) - 1, VMEM),
            out_specs=(pl.BlockSpec(memory_space=VMEM),) * len(outs),
            scratch_shapes=[
                SMEM((2 * padded, width), jnp.int32),
                SMEM(lengths.shape, jnp.int32),
                VMEM((padded, width), jnp.float32),
                pltpu.SemaphoreType.DMA((2,)),
            ],
            compiler_params=LIMIT,
            cost_estimate=pl.CostEstimate(flops=3 * 10**9, bytes_accessed=0, transcendentals=0),
            name="pairs",
        )(*operands)
        return out[0][:, : blocks * picks], out[1:]

    steps = []
    d = shards // 2
    while d >= 1:
        steps.append(d)
        d //= 2
    unit = 2 * WIDE
    units = passages // unit
    parts = len(steps)
    cuts = [(2 * units * i + parts) // (2 * parts) * unit for i in range(parts + 1)]
    held = payload[None]
    wide = embedded = None
    for i, d in enumerate(steps[:-2]):
        moved = swap_shard(held, d)
        if cuts[i] < cuts[i + 1]:
            embedded, wide = decode(cuts[i], cuts[i + 1], wide, embedded)
            moved, embedded = lax.optimization_barrier((moved, embedded))
        held = jnp.concatenate([held, moved], axis=0)
    moved = swap_shard(held, steps[-2])
    far_a = swap_shard(held, 1)
    if cuts[-3] < cuts[-2]:
        embedded, wide = decode(cuts[-3], cuts[-2], wide, embedded)
        moved, embedded = lax.optimization_barrier((moved, embedded))
    far_b = swap_shard(moved, 1)
    near = jnp.concatenate([held, moved], axis=0)
    near_other = swap_sub(near)
    embedded, wide = decode(cuts[-2], cuts[-1], wide, embedded)
    far_b, embedded = lax.optimization_barrier((far_b, embedded))
    far = jnp.concatenate([far_a, far_b], axis=0)
    far_scores, near_found = score(find(far), far, swap_sub(far), near)
    near_scores, _ = score(near_found, near, near_other)
    total = near_scores + swap_shard(far_scores, 1)
    for d in reversed(steps[2:-1]):
        half = total.shape[1] // 2
        total = total[:, :half] + swap_shard(total[:, half:], d)
    far_d, near_d = steps[:2]
    core = lax.axis_index("sub")

    def swap_apart(x, even, odd):
        count = shards * halves
        pairs = [(i, i ^ (halves * (odd if i % 2 else even))) for i in range(count)]
        return lax.ppermute(x, ("shard", "sub"), pairs)

    total = total + swap_sub(total)
    mine, to_far, to_near, to_both = (total[:, i * picks : (i + 1) * picks] for i in range(4))
    one = swap_apart(jnp.where(core == 1, to_far, to_near), near_d, far_d)
    two = swap_apart(to_both, 1, far_d ^ near_d)
    part = one + jnp.where(core == 1, two, mine)
    return part + swap_sub(part)


def solution(mesh):
    return jax.shard_map(
        body,
        mesh=mesh,
        in_specs=(
            P(("groups", "shard"), "sub", None),
            P(("groups", "shard"), None),
            P(("shard", "sub"), None, None),
            P(("shard", "sub"), None),
            P(("shard", "sub"), None),
            P(("shard", "sub")),
            P(),
            P(),
        ),
        out_specs=P(("groups", "shard"), None),
        check_vma=False,
    )
```

```python
import functools
import math

import jax
import jax.numpy as jnp
from jax import lax
from jax.experimental import pallas as pl
from jax.experimental.pallas import tpu as pltpu
from jax.sharding import PartitionSpec as P

masked_floor = -1000000000.0
UNROLLED = 128
VMEM = pltpu.VMEM
SMEM = pltpu.SMEM
LIMIT = pltpu.CompilerParams(vmem_limit_bytes=40 * 2**20)


def iota(shape, dim):
    return lax.broadcasted_iota(jnp.int32, shape, dim)


def ones_where(mask):
    return jnp.where(mask, 1.0, 0.0).astype(jnp.bfloat16)


def dot(a, b, contract=((1,), (0,))):
    return lax.dot_general(a, b, (contract, ((), ())), preferred_element_type=jnp.float32)


def spread(feature, words, per):
    return per * (feature % words) + feature // words


def order_kernel(words, out_ref):
    width = out_ref.shape[0]
    source = spread(iota((width, width), 1), words, width // words)
    out_ref[...] = ones_where(iota((width, width), 0) == source)


def pack_kernel(passages, query_ref, cand_ref, order_ref, out_ref):
    count, tokens, width = query_ref.shape
    picks = cand_ref.shape[1]
    flat = query_ref[...].reshape(count * tokens, width)
    rows = count * tokens
    out_ref[0:rows, :] = dot(flat, order_ref[...]).astype(jnp.bfloat16)
    ids = cand_ref[...]
    owner = ids // passages
    local = ids - owner * passages
    row = iota((picks, width), 0)
    lane = iota((picks, width), 1)
    tile = jnp.zeros((count, width), jnp.float32)
    for i, part in enumerate((owner, local)):
        place = ones_where(lane == row + i * picks)
        tile += dot(part.astype(jnp.float32).astype(jnp.bfloat16), place)
    out_ref[rows : rows + count, :] = tile.astype(jnp.bfloat16)


def slot_kernel(queries, picks, capacity, rows_ref, slot_ref, rank_ref):
    blocks = rows_ref.shape[0]
    width = rows_ref.shape[2]
    body_rows = rows_ref.shape[1] - queries
    groups = width // picks
    rows = blocks * queries
    me = lax.axis_index("shard") * lax.axis_size("sub") + lax.axis_index("sub")
    ids = rows_ref[:, body_rows:, :].reshape(rows, width)
    li = iota((width, width), 0)
    lj = iota((width, width), 1)
    owner = dot(ids, ones_where(li == lj % picks))
    local = dot(ids, ones_where(li == picks + lj % picks))
    here = owner == jnp.full((rows, width), me, jnp.int32).astype(jnp.float32)
    here_bf = ones_where(here)
    before_lane = ones_where((li < picks) & (li < lj % picks))
    whole_row = ones_where(li < picks)
    ri = iota((rows, rows), 0)
    rj = iota((rows, rows), 1)
    before_row = ones_where((ri // queries == rj // queries) & (rj < ri))
    totals = dot(here_bf, whole_row).astype(jnp.bfloat16)
    rank = dot(here_bf, before_lane) + dot(before_row, totals)
    rank = rank.astype(jnp.int32)
    rank_ref[...] = jnp.where(here, rank, -1)
    lane_group = iota((rows, width), 1) // picks
    which = (iota((rows, width), 0) % queries).astype(jnp.float32)
    padded = slot_ref.shape[0] // 2
    collect = ones_where(iota((padded, rows), 0) == iota((padded, rows), 1) // queries)
    slot_q = jnp.zeros((padded, width), jnp.float32)
    slot_p = jnp.zeros((padded, width), jnp.float32)
    for i in range(-(-capacity // groups)):
        chosen = here & (rank == i * groups + lane_group)
        to_slot = ones_where(lj == i * groups + li // picks)
        got_q = dot(collect, jnp.where(chosen, which, 0.0).astype(jnp.bfloat16))
        got_p = dot(collect, jnp.where(chosen, local, 0.0).astype(jnp.bfloat16))
        slot_q += dot(got_q.astype(jnp.bfloat16), to_slot)
        slot_p += dot(got_p.astype(jnp.bfloat16), to_slot)
    slot_ref[0:padded, :] = slot_q.astype(jnp.int32)
    slot_ref[padded : 2 * padded, :] = slot_p.astype(jnp.int32)


WIDE = 4


def decode_kernel(first, start, stop, *refs):
    refs = list(refs)
    ids_all, words_ref, scale_bf, bucket_ref = refs[:4]
    del refs[:4]
    if first:
        table_ref = refs.pop(0)
    else:
        wide = refs.pop(0)
        refs.pop(0)
    out_ref = refs.pop(0)
    if first:
        wide = refs.pop(0)
    rows, ids_ref, scale_ref, sem = refs
    copy = pltpu.make_async_copy(ids_all.at[pl.ds(start, stop - start)], ids_ref, sem)
    copy.start()
    scale_ref[...] = scale_bf[...].astype(jnp.float32)
    if first:
        chunk = 512

        def widen(j, _):
            r = pl.ds(pl.multiple_of(j * chunk, chunk), chunk)
            wide[r, :] = table_ref[r, :].astype(jnp.float32)
            return 0

        lax.fori_loop(0, table_ref.shape[0] // chunk, widen, 0)
    copy.wait()
    slots = ids_ref.shape[1]
    width = wide.shape[1]
    words = words_ref.shape[1]
    per = width // words
    order = ones_where(iota((width, width), 1) == spread(iota((width, width), 0), words, per))
    levels = [
        jnp.broadcast_to(bucket_ref[0:1, i : i + 1].astype(jnp.float32), (words, slots * WIDE))
        for i in range(4)
    ]

    def fetch(p, buf):
        for u in range(WIDE):
            for g in range(slots // 16):
                got = jnp.concatenate(
                    [wide[pl.ds(ids_ref[p + u, g * 16 + i], 1), :] for i in range(16)], axis=0
                )
                r = u * slots + g * 16
                rows[buf, r : r + 16, :] = got.astype(jnp.bfloat16)
                yield

    def build(p, buf, fetching):
        packed = jnp.concatenate([words_ref[start + p + u] for u in range(WIDE)], axis=1)
        centre = dot(order, rows[buf], ((1,), (1,)))
        parts = []
        for k in range(per):
            for _ in range(WIDE):
                next(fetching, None)
            low = (packed & (1 << (2 * k))) != 0
            high = (packed & (2 << (2 * k))) != 0
            parts.append(
                jnp.where(
                    high,
                    jnp.where(low, levels[3], levels[2]),
                    jnp.where(low, levels[1], levels[0]),
                )
            )
        value = jnp.concatenate(parts, axis=0)
        scale = jnp.concatenate([scale_ref[pl.ds(start + p + u, 1), :] for u in range(WIDE)], axis=1)
        raw = centre + scale * value
        inverse = lax.rsqrt(jnp.sum(raw * raw, axis=0, keepdims=True) + 1e-06)
        out = (raw * inverse).astype(jnp.bfloat16)
        for u in range(WIDE):
            out_ref[start + p + u] = out[:, u * slots : (u + 1) * slots]
        for _ in fetching:
            pass

    for _ in fetch(0, 0):
        pass

    def step(i, _):
        p = 2 * WIDE * i
        build(p, 0, fetch(p + WIDE, 1))
        build(p + WIDE, 1, fetch(p + 2 * WIDE, 0))
        return 0

    last = stop - start - 2 * WIDE
    for i in range(last // (2 * WIDE)):
        step(i, 0)
    build(last, 0, fetch(last + WIDE, 1))
    build(last + WIDE, 1, iter(()))


def pair_kernel(queries, picks, capacity, ahead, len_hbm, slot_ref, rank_ref, mine_ref, other_ref, emb_ref, *refs):
    refs = list(refs)
    if ahead:
        later_ref = refs.pop(0)
    out_ref = refs.pop(0)
    later_out = refs[: 2 * ahead]
    slot_s, len_s, score, sems = refs[2 * ahead :]
    copies = [
        pltpu.make_async_copy(slot_ref, slot_s, sems.at[0]),
        pltpu.make_async_copy(len_hbm, len_s, sems.at[1]),
    ]
    for c in copies:
        c.start()
    if ahead:
        slot_kernel(queries, picks, capacity, later_ref, *later_out)
    for c in copies:
        c.wait()
    blocks = mine_ref.shape[0]
    width = mine_ref.shape[2]
    tokens = (mine_ref.shape[1] - queries) // queries
    padded = slot_s.shape[0] // 2
    full_tokens = 2 * tokens
    slots = emb_ref.shape[2]
    lane = iota((full_tokens, slots), 1)
    spot = iota((full_tokens, width), 1)

    def block(b):
        best_all = jnp.zeros((full_tokens, width), jnp.float32)
        for s in range(0, capacity, 2):
            asked = []
            kept = []
            stored = []
            for j in range(s, s + 2):
                p = slot_s[padded + b, j]
                r = pl.ds(pl.multiple_of(slot_s[b, j] * tokens, tokens), tokens)
                asked += [mine_ref[b, r, :], other_ref[b, r, :]]
                stored.append(emb_ref[p])
                kept.append(len_s[p])
            both = dot(jnp.concatenate(asked, axis=0), jnp.concatenate(stored, axis=1))
            for j in range(2):
                similar = both[j * full_tokens : (j + 1) * full_tokens, j * slots : (j + 1) * slots]
                similar = jnp.where(lane < kept[j], similar, masked_floor)
                best = jnp.max(similar, axis=1, keepdims=True)
                best_all = jnp.where(spot == s + j, best, best_all)
        score[pl.ds(b, 1), :] = jnp.sum(best_all, axis=0, keepdims=True) * (1.0 / full_tokens)

    together = math.gcd(blocks, max(1, UNROLLED // capacity))

    def several(i, _):
        for u in range(together):
            block(i * together + u)
        return 0

    lax.fori_loop(0, blocks // together, several, 0)
    groups = width // picks
    lane_group = iota((queries, width), 1) // picks
    for c in range(0, blocks, groups):
        out = jnp.zeros((queries, width), jnp.float32)
        for b in range(c, min(c + groups, blocks)):
            rank = rank_ref[b * queries : (b + 1) * queries, :]
            line = jnp.broadcast_to(score[b : b + 1, :], (queries, width))
            line = jnp.take_along_axis(line, jnp.maximum(rank, 0), axis=1)
            out = jnp.where((rank >= 0) & (lane_group == b - c), line, out)
        out_ref[:, c * picks : c * picks + width] = out


def whole(n, *spaces):
    return [pl.BlockSpec(memory_space=s) for s in spaces] * n


def body(queries, candidates, residuals, centroid_ids, block_scales, lengths, centroids, bucket_weights):
    shards = lax.axis_size("shard")
    halves = lax.axis_size("sub")
    query_count, picks = candidates.shape
    tokens, width = queries.shape[1:]
    passages, slots, words = residuals.shape
    capacity = max(2, 2 * query_count * picks // (shards * halves))

    def swap_shard(x, d):
        return lax.ppermute(x, "shard", [(i, i ^ d) for i in range(shards)])

    def swap_sub(x):
        return lax.ppermute(x, "sub", [(i, i ^ 1) for i in range(halves)])

    order = pl.pallas_call(
        functools.partial(order_kernel, words),
        out_shape=jax.ShapeDtypeStruct((width, width), jnp.bfloat16),
        out_specs=pl.BlockSpec(memory_space=VMEM),
        compiler_params=LIMIT,
        cost_estimate=pl.CostEstimate(flops=6 * 10**9, bytes_accessed=0, transcendentals=0),
        name="order",
    )()
    payload = pl.pallas_call(
        functools.partial(pack_kernel, passages),
        out_shape=jax.ShapeDtypeStruct((query_count * (tokens + 1), width), jnp.bfloat16),
        in_specs=whole(3, VMEM),
        out_specs=pl.BlockSpec(memory_space=VMEM),
        compiler_params=LIMIT,
        cost_estimate=pl.CostEstimate(flops=6 * 10**9, bytes_accessed=0, transcendentals=0),
        name="pack",
    )(queries, candidates, order)

    stored = (
        centroid_ids,
        jnp.swapaxes(residuals, 1, 2),
        block_scales,
        bucket_weights.reshape(1, 4),
    )
    emb_shape = jax.ShapeDtypeStruct((passages, width, slots), jnp.bfloat16)
    wide_shape = jax.ShapeDtypeStruct(centroids.shape, jnp.float32)

    def slot_shapes(blocks):
        padded = -(-blocks // 8) * 8
        return (
            jax.ShapeDtypeStruct((2 * padded, width), jnp.int32),
            jax.ShapeDtypeStruct((blocks * query_count, width), jnp.int32),
        )

    def decode(start, stop, wide, embedded):
        first = embedded is None
        extra = (centroids,) if first else (wide, embedded)
        outs = (emb_shape, wide_shape) if first else (emb_shape,)
        specs = whole(4 + len(extra), VMEM)
        out = pl.pallas_call(
            functools.partial(decode_kernel, first, start, stop),
            out_shape=outs,
            in_specs=specs,
            out_specs=(pl.BlockSpec(memory_space=VMEM),) * len(outs),
            scratch_shapes=[
                VMEM((2, WIDE * slots, width), jnp.bfloat16),
                SMEM((stop - start, slots), jnp.int32),
                VMEM(block_scales.shape, jnp.float32),
                pltpu.SemaphoreType.DMA,
            ],
            input_output_aliases={} if first else {5: 0},
            compiler_params=LIMIT,
            cost_estimate=pl.CostEstimate(
                flops=(stop - start) * 2 * 10**8, bytes_accessed=0, transcendentals=0
            ),
            name="decode",
        )(*stored, *extra)
        return out[0], out[1] if first else wide

    def find(mine):
        return pl.pallas_call(
            functools.partial(slot_kernel, query_count, picks, capacity),
            out_shape=slot_shapes(mine.shape[0]),
            in_specs=whole(1, VMEM),
            out_specs=(pl.BlockSpec(memory_space=VMEM),) * 2,
            compiler_params=LIMIT,
            cost_estimate=pl.CostEstimate(flops=10**9, bytes_accessed=0, transcendentals=0),
            name="slots",
        )(mine)

    def score(found, mine, other, later=None):
        blocks = mine.shape[0]
        padded = -(-blocks // 8) * 8
        lanes = -(-blocks * picks // width) * width
        outs = (jax.ShapeDtypeStruct((query_count, lanes), jnp.float32),)
        operands = (lengths, *found, mine, other, embedded)
        if later is not None:
            outs += slot_shapes(later.shape[0])
            operands += (later,)
        out = pl.pallas_call(
            functools.partial(pair_kernel, query_count, picks, capacity, later is not None),
            out_shape=outs,
            in_specs=whole(1, pltpu.HBM) + whole(len(operands) - 1, VMEM),
            out_specs=(pl.BlockSpec(memory_space=VMEM),) * len(outs),
            scratch_shapes=[
                SMEM((2 * padded, width), jnp.int32),
                SMEM(lengths.shape, jnp.int32),
                VMEM((padded, width), jnp.float32),
                pltpu.SemaphoreType.DMA((2,)),
            ],
            compiler_params=LIMIT,
            cost_estimate=pl.CostEstimate(flops=3 * 10**9, bytes_accessed=0, transcendentals=0),
            name="pairs",
        )(*operands)
        return out[0][:, : blocks * picks], out[1:]

    steps = []
    d = shards // 2
    while d >= 1:
        steps.append(d)
        d //= 2
    unit = 2 * WIDE
    units = passages // unit
    parts = len(steps)
    cuts = [(2 * units * i + parts) // (2 * parts) * unit for i in range(parts + 1)]
    held = payload[None]
    wide = embedded = None
    for i, d in enumerate(steps[:-2]):
        moved = swap_shard(held, d)
        if cuts[i] < cuts[i + 1]:
            embedded, wide = decode(cuts[i], cuts[i + 1], wide, embedded)
            moved, embedded = lax.optimization_barrier((moved, embedded))
        held = jnp.concatenate([held, moved], axis=0)
    moved = swap_shard(held, steps[-2])
    far_a = swap_shard(held, 1)
    if cuts[-3] < cuts[-2]:
        embedded, wide = decode(cuts[-3], cuts[-2], wide, embedded)
        moved, embedded = lax.optimization_barrier((moved, embedded))
    far_b = swap_shard(moved, 1)
    near = jnp.concatenate([held, moved], axis=0)
    near_other = swap_sub(near)
    embedded, wide = decode(cuts[-2], cuts[-1], wide, embedded)
    far_b, embedded = lax.optimization_barrier((far_b, embedded))
    far = jnp.concatenate([far_a, far_b], axis=0)
    far_scores, near_found = score(find(far), far, swap_sub(far), near)
    near_scores, _ = score(near_found, near, near_other)
    total = near_scores + swap_shard(far_scores, 1)
    for d in reversed(steps[2:-1]):
        half = total.shape[1] // 2
        total = total[:, :half] + swap_shard(total[:, half:], d)
    far_d, near_d = steps[:2]
    core = lax.axis_index("sub")

    def swap_apart(x, even, odd):
        count = shards * halves
        pairs = [(i, i ^ (halves * (odd if i % 2 else even))) for i in range(count)]
        return lax.ppermute(x, ("shard", "sub"), pairs)

    total = total + swap_sub(total)
    mine, to_far, to_near, to_both = (total[:, i * picks : (i + 1) * picks] for i in range(4))
    one = swap_apart(jnp.where(core == 1, to_both, to_near), near_d, far_d ^ near_d)
    two = swap_apart(to_far, 1, far_d)
    part = one + jnp.where(core == 1, two, mine)
    return part + swap_sub(part)


def solution(mesh):
    return jax.shard_map(
        body,
        mesh=mesh,
        in_specs=(
            P(("groups", "shard"), "sub", None),
            P(("groups", "shard"), None),
            P(("shard", "sub"), None, None),
            P(("shard", "sub"), None),
            P(("shard", "sub"), None),
            P(("shard", "sub")),
            P(),
            P(),
        ),
        out_specs=P(("groups", "shard"), None),
        check_vma=False,
    )
```
